512 devices in a mesh: ctx: 64 (over z, y_hi, core), tp: 8 (over x, y_lo).
Axes of the slice: x: 4, y: 8 (y_hi: 4, y_lo: 2; y = y_hi * 2 + y_lo), z: 8, core: 2. Of those that a mesh axis runs over, the one named last changes fastest.
Arguments:
- queries: bfloat16 [12288, 4096], P('ctx', 'tp'), may hold values from -21 to 21
- keys: bfloat16 [12288, 1024], P('ctx', 'tp'), may hold values from -6 to 6
- values: bfloat16 [12288, 1024], P('ctx', 'tp'), may hold values from -6 to 6
- row_route: int32 [12288], P('ctx'), may hold values from 0 to 12287, as said below
- lengths: int32 [16], replicated, may hold values from 1 to 3072, 12288 in all
Outputs:
- attended: bfloat16 [12288, 4096], P('ctx', 'tp')
The draws below stay inside these ranges and needn't reach their ends.
Inputs may be any that keep to these rules, and one draw needn't show every extreme that they name: `row_route`: A permutation of the output rows. The rows of one loader device bound for one rank (output rows r * 192 to (r + 1) * 192 - 1) number at most 6, exactly 6 for some rank; every loader device sends the same multiset of counts over the ranks, and every rank receives that multiset.
All inputs are finite; a program needn't handle non-finite values.
Results may differ from the reference program's by a relative error of at most 0.0065.
Values may be sent and summed in bfloat16 or wider, within the bound.
No kernel may reach another device: no remote copies, remote signals or barrier semaphores. Data moves between devices by JAX's collectives and lax.ppermute only.
A program may use at most 128 MiB of HBM per device.

```python
import math
import jax
import jax.numpy as jnp
import numpy as np
from jax import lax

QUERY_HEADS = 32
KEY_VALUE_HEADS = 8
HEAD_WIDTH = 128
TOKENS_PER_RANK = 192
DOCS = 16
PACKED_TOKENS = 12288
CAP = 6
N_CTX = 64


def route_table(key):
    key = jax.random.fold_in(key, 11)
    key_sizes, key_offsets, key_left, key_right = jax.random.split(key, 4)
    spread = jax.random.randint(key_sizes, (N_CTX // 2,), 0, CAP // 2 + 1).astype(jnp.int32)
    spread = spread.at[0].set(CAP // 2)
    round_sizes = jnp.stack([CAP // 2 + spread, CAP // 2 - spread], axis=1).reshape(N_CTX)
    round_ends = jnp.cumsum(round_sizes).astype(jnp.int32)
    ordinal = jnp.arange(TOKENS_PER_RANK, dtype=jnp.int32)
    round_index = jnp.sum((ordinal[:, None] >= round_ends[None, :]).astype(jnp.int32), axis=1)
    offsets = jax.random.permutation(key_offsets, N_CTX).astype(jnp.int32)
    loaders = jnp.arange(N_CTX, dtype=jnp.int32)
    target = (loaders[:, None] + offsets[round_index][None, :]) % N_CTX
    left_perm = jax.vmap(lambda subkey: jax.random.permutation(subkey, TOKENS_PER_RANK))(jax.random.split(key_left, N_CTX)).astype(jnp.int32)
    right_perm = jax.vmap(lambda subkey: jax.random.permutation(subkey, TOKENS_PER_RANK))(jax.random.split(key_right, N_CTX)).astype(jnp.int32)
    destination = target * TOKENS_PER_RANK + right_perm[target, jnp.broadcast_to(ordinal[None, :], target.shape)]
    where_rows = loaders[:, None] * TOKENS_PER_RANK + left_perm
    return jnp.zeros((PACKED_TOKENS,), jnp.int32).at[where_rows.reshape(-1)].set(destination.reshape(-1).astype(jnp.int32))


def query_key_pair(key):
    key = jax.random.fold_in(key, 23)
    key_q, key_k = jax.random.split(key, 2)
    q_shape = (PACKED_TOKENS, QUERY_HEADS * HEAD_WIDTH)
    key_layout = (PACKED_TOKENS, KEY_VALUE_HEADS * HEAD_WIDTH)
    q_full = jnp.clip(jax.random.normal(key_q, q_shape, jnp.float32), -6.0, 6.0)
    complete_keys = jnp.clip(jax.random.normal(key_k, key_layout, jnp.float32), -6.0, 6.0)
    return (q_full, complete_keys)


def draw_row_route(key, part):
    return route_table(key)


def draw_queries(key, part):
    q_full, complete_keys = query_key_pair(key)
    return q_full.astype(jnp.bfloat16)


def draw_keys(key, part):
    q_full, complete_keys = query_key_pair(key)
    return complete_keys.astype(jnp.bfloat16)


def block_scale(stream_key, shape, cuts, low, largest):
    factor_of, own = 1.0, jax.random.fold_in(stream_key, 6)
    for position, parts in cuts:
        steps = jnp.exp(jax.random.uniform(jax.random.fold_in(own, position), (parts,), jnp.float32, low / len(cuts), largest / len(cuts)))
        factor_of = factor_of * jnp.repeat(steps, shape[position] // parts).reshape([-1 if axis == position else 1 for axis in range(len(shape))])
    return factor_of


def split_up(count, total, bound, slope):
    loads = [(1 << 20) // math.isqrt(grade ** slope) + 1 for grade in range(2, count + 1)]
    surplus, holding = total - bound - (count - 1), [1] * (count - 1)
    while surplus > 0:
        free = [i for i in range(count - 1) if holding[i] < bound]
        mass, left = sum([loads[i] for i in free]), surplus
        for i in free:
            more = min(bound - holding[i], max(1, left * loads[i] // mass), surplus)
            holding[i] = holding[i] + more
            surplus = surplus - more
    return np.array([bound] + holding)


def ragged(rng, count, total, most, skew):
    if count == 2:
        one = jax.random.randint(rng, (), max(1, total - most), min(most, total - 1) + 1)
        return jnp.stack([one, total - one])
    sizes = jnp.asarray(split_up(count, total, most, skew), jnp.int32)
    twos = (count - 1) // 2
    source_of, sink = sizes[1:1 + 2 * twos:2], sizes[2:2 + 2 * twos:2]
    room = jnp.minimum(source_of - 1, most - sink)
    moved = jax.random.randint(jax.random.fold_in(rng, 1), (twos,), 0, 1 << 20) % (room + 1)
    sizes = sizes.at[1:1 + 2 * twos:2].set(source_of - moved).at[2:2 + 2 * twos:2].set(sink + moved)
    return sizes[jax.random.permutation(jax.random.fold_in(rng, 2), count)]


def gaussian(key, extent, deviation, most, cuts=(), kind=jnp.bfloat16):
    loudness = block_scale(key, extent, cuts, -0.22, 0.18) if cuts else 1.0
    values = jax.random.normal(key, extent, jnp.float32) * deviation * loudness
    return jnp.minimum(jnp.maximum(values, -most), most).astype(kind)


def setup_inputs(seed: int = 0) -> dict:
    seeds = jax.random.split(jax.random.key(seed), 6)
    queries = draw_queries(jax.random.fold_in(seeds[5], 71), 0)
    keys = draw_keys(jax.random.fold_in(seeds[5], 71), 0)
    values = gaussian(seeds[2], (PACKED_TOKENS, KEY_VALUE_HEADS * HEAD_WIDTH), 1.0, 6.0, ((0, 64), (1, 8)))
    row_route = draw_row_route(jax.random.fold_in(seeds[5], 71), 0)
    lengths = ragged(seeds[4], DOCS, PACKED_TOKENS, PACKED_TOKENS // 4, 2).astype(jnp.int32)
    return dict(queries=queries, keys=keys, values=values, row_route=row_route, lengths=lengths)


def slot_position(row_ids, tok_dev, ranks_count):
    half_rows = tok_dev // 2
    owner = row_ids // tok_dev
    slot_id = row_ids - owner * tok_dev
    return jnp.where(slot_id < half_rows, owner * half_rows + slot_id,
                     (2 * ranks_count - 1 - owner) * half_rows + slot_id - half_rows).astype(jnp.int32)


def document_of(positions, lengths):
    boundary = jnp.cumsum(lengths).astype(jnp.int32)
    return jnp.sum((positions[:, None] >= boundary[None, :]).astype(jnp.int32), axis=1)


def reference(queries, keys, values, row_route, lengths):
    rows_all = jnp.arange(PACKED_TOKENS, dtype=jnp.int32)
    sender_rank = jnp.zeros((PACKED_TOKENS,), jnp.int32).at[row_route].set(rows_all)
    q_sorted = queries[sender_rank]
    heads_of_key = keys[sender_rank].reshape(PACKED_TOKENS, KEY_VALUE_HEADS, HEAD_WIDTH).astype(jnp.float32)
    heads_of_value = values[sender_rank].reshape(PACKED_TOKENS, KEY_VALUE_HEADS, HEAD_WIDTH).astype(jnp.float32)
    positions = slot_position(rows_all, TOKENS_PER_RANK, N_CTX)
    doc_ids = document_of(positions, lengths)
    query_groups = QUERY_HEADS // KEY_VALUE_HEADS

    def one_block(block_id):
        first_row = (block_id * TOKENS_PER_RANK).astype(jnp.int32)
        query_block = lax.dynamic_slice_in_dim(q_sorted, first_row, TOKENS_PER_RANK, 0)
        query_block = query_block.reshape(TOKENS_PER_RANK, KEY_VALUE_HEADS, query_groups, HEAD_WIDTH).astype(jnp.float32)
        query_pos = lax.dynamic_slice_in_dim(positions, first_row, TOKENS_PER_RANK, 0)
        query_doc = lax.dynamic_slice_in_dim(doc_ids, first_row, TOKENS_PER_RANK, 0)
        scores = jnp.einsum("tkgd,skd->kgts", query_block, heads_of_key) * (HEAD_WIDTH ** -0.5)
        allowed = (query_doc[:, None] == doc_ids[None, :]) & (positions[None, :] <= query_pos[:, None])
        masked = jnp.where(allowed, scores, -jnp.inf)
        row_max = jnp.max(masked, axis=3, keepdims=True)
        weight = jnp.exp(masked - row_max)
        summed = jnp.sum(weight, axis=3)
        rounded = weight.astype(jnp.bfloat16).astype(jnp.float32)
        result = jnp.einsum("kgts,skd->kgtd", rounded, heads_of_value) / summed[..., None]
        return result.transpose(2, 0, 1, 3).reshape(TOKENS_PER_RANK, QUERY_HEADS * HEAD_WIDTH).astype(jnp.bfloat16)

    blocks = lax.map(one_block, jnp.arange(N_CTX, dtype=jnp.int32))
    return blocks.reshape(PACKED_TOKENS, QUERY_HEADS * HEAD_WIDTH)
```

```python
import functools
import math

import jax
import jax.numpy as jnp
from jax import lax
from jax.experimental import pallas as pl
from jax.experimental.pallas import tpu as pltpu
from jax.sharding import PartitionSpec as P

HEAD_WIDTH = 128
CAP = 12
SLOTS = 16
NEG = -1e30
VMEM = pl.BlockSpec(memory_space=pltpu.VMEM)
SMEM = pl.BlockSpec(memory_space=pltpu.SMEM)


def iota(shape, dim):
    return lax.broadcasted_iota(jnp.int32, shape, dim)


def pack_kernel(n, route_ref, k_ref, v_ref, kv_ref, pick_ref):
    tok = k_ref.shape[0]
    half = tok // 2
    rows = n * SLOTS
    route = route_ref[...]
    owner = jnp.zeros_like(route)
    owner = ((route.astype(jnp.float32) + 0.5) * (1.0 / tok)).astype(jnp.int32)
    slot = route - owner * tok
    pos = jnp.where(slot < half, owner * half + slot, (2 * n - 1 - owner) * half + slot - half)
    chunk = ((pos.astype(jnp.float32) + 0.5) * (1.0 / tok)).astype(jnp.int32)
    place = pos - chunk * tok
    square = (tok, tok)
    down, across = iota(square, 0), iota(square, 1)
    chunk_rows = jnp.broadcast_to(chunk, square)
    chunk_col = jnp.sum(jnp.where(down == across, chunk_rows, 0), axis=1, keepdims=True)
    earlier = jnp.where((chunk_col == chunk_rows) & (down < across), 1, 0)
    order = jnp.sum(earlier, axis=0, keepdims=True)
    where_to = chunk * SLOTS + order
    wide = (rows, tok)
    line = iota(wide, 0)
    one, zero = jnp.float32(1), jnp.float32(0)
    pick = jnp.where(line == jnp.broadcast_to(where_to, wide), one, zero).astype(jnp.bfloat16)
    pick_ref[...] = pick
    mark = jnp.where(line == jnp.broadcast_to(chunk * SLOTS + CAP, wide), one, zero).astype(
        jnp.bfloat16
    )
    lanes = (HEAD_WIDTH, tok)
    places = jnp.where(
        iota(lanes, 0) == jnp.broadcast_to(order, lanes),
        jnp.broadcast_to(place + 1, lanes).astype(jnp.float32),
        zero,
    ).astype(jnp.bfloat16)
    packed_k = jnp.dot(pick, k_ref[...], preferred_element_type=jnp.float32)
    packed_k += lax.dot_general(
        mark, places, (((1,), (1,)), ((), ())), preferred_element_type=jnp.float32
    )
    kv_ref[:, :HEAD_WIDTH] = packed_k.astype(jnp.bfloat16)
    kv_ref[:, HEAD_WIDTH:] = jnp.dot(
        pick, v_ref[...], preferred_element_type=jnp.float32
    ).astype(jnp.bfloat16)


def unpack_kernel(n, got_ref, kv_ref, pick_ref):
    tok = kv_ref.shape[0]
    rows = n * SLOTS
    one, zero = jnp.float32(1), jnp.float32(0)
    tall = (n, rows)
    chooser = jnp.where(iota(tall, 1) == iota(tall, 0) * SLOTS + CAP, one, zero).astype(
        jnp.bfloat16
    )
    places = jnp.dot(chooser, got_ref[:, :HEAD_WIDTH], preferred_element_type=jnp.float32)
    lanes = (HEAD_WIDTH, rows)
    spread = jnp.where((iota(lanes, 1) & (SLOTS - 1)) == iota(lanes, 0), one, zero).astype(
        jnp.bfloat16
    )
    across = jnp.dot(places.astype(jnp.bfloat16), spread, preferred_element_type=jnp.float32)
    mine = iota(tall, 1) - iota(tall, 0) * SLOTS
    place = jnp.sum(
        jnp.where((mine >= 0) & (mine < CAP), across, zero), axis=0, keepdims=True
    )
    wide = (tok, rows)
    pick = jnp.where(
        (iota(wide, 0) + 1).astype(jnp.float32) == jnp.broadcast_to(place, wide), one, zero
    ).astype(jnp.bfloat16)
    pick_ref[...] = pick
    kv_ref[...] = jnp.dot(pick, got_ref[...], preferred_element_type=jnp.float32).astype(
        jnp.bfloat16
    )


def attend_kernel(
    groups, lengths_ref, index_ref, pick_ref, q_ref, own_ref, *rest
):
    far_refs, (first_ref, second_ref, heads_ref) = rest[:4], rest[4:]
    tok = pick_ref.shape[0]
    half = tok // 2
    span = 2 * tok
    index = index_ref[0]
    chip = index // 2
    scale = HEAD_WIDTH ** (-0.5) * math.log2(math.e)

    for g in range(groups):
        heads_ref[g * tok : (g + 1) * tok, :] = jnp.dot(
            pick_ref[...],
            q_ref[:, g * HEAD_WIDTH : (g + 1) * HEAD_WIDTH],
            preferred_element_type=jnp.float32,
        ).astype(jnp.bfloat16)

    wide = (tok, span)
    query_pos = index * tok + iota(wide, 0)
    start = jnp.zeros(wide, jnp.int32)
    first_start = jnp.int32(0)
    end = jnp.int32(0)
    for i in range(lengths_ref.shape[0]):
        end = end + lengths_ref[i]
        start = jnp.where(query_pos >= end, end, start)
        first_start = jnp.where(index * tok >= end, end, first_start)

    def block(keys, values, base, state, last):
        key_pos = base + iota(wide, 1)
        allowed = key_pos >= start
        if last:
            allowed = allowed & (key_pos <= query_pos)
        out = []
        for g in range(groups):
            s = lax.dot_general(
                heads_ref[g * tok : (g + 1) * tok, :],
                keys,
                (((1,), (1,)), ((), ())),
                preferred_element_type=jnp.float32,
            )
            s = jnp.where(allowed, s * scale, NEG)
            top = jnp.max(s, axis=1, keepdims=True)
            if state is not None:
                top = jnp.maximum(top, state[3 * g])
            w = jnp.exp2(s - top)
            total = jnp.sum(w, axis=1, keepdims=True)
            acc = jnp.dot(w.astype(jnp.bfloat16), values, preferred_element_type=jnp.float32)
            if state is not None:
                keep = jnp.exp2(state[3 * g] - top)
                total += state[3 * g + 1] * keep
                acc += state[3 * g + 2] * keep
            out += [top, total, acc]
        return tuple(out)

    state = block(
        own_ref[:, :HEAD_WIDTH], own_ref[:, HEAD_WIDTH:], chip * span, None, True
    )
    for distance in range(1, 9):
        ref = far_refs[(distance - 1) // 2]
        low = ((distance - 1) % 2) * span
        base = (chip - distance) * span
        needed = (chip >= distance) & (base + span > first_start)
        state = lax.cond(
            needed,
            lambda st, ref=ref, low=low, base=base: block(
                ref[low : low + span, :HEAD_WIDTH],
                ref[low : low + span, HEAD_WIDTH:],
                base,
                st,
                False,
            ),
            lambda st: st,
            state,
        )
    for g in range(groups):
        lanes = slice(g * HEAD_WIDTH, (g + 1) * HEAD_WIDTH)
        out = (state[3 * g + 2] / state[3 * g + 1]).astype(jnp.bfloat16)
        first_ref[:, lanes] = out[:half]
        second_ref[:, lanes] = out[half:]


def local(queries, keys, values, row_route, lengths):
    n = lax.axis_size("ctx")
    index = lax.axis_index("ctx")
    tok, width = queries.shape
    groups = width // HEAD_WIDTH
    rows = n * SLOTS
    params = pltpu.CompilerParams(vmem_limit_bytes=48 * 2**20)
    bf16 = jnp.bfloat16

    packed_kv, pick = pl.pallas_call(
        functools.partial(pack_kernel, n),
        out_shape=(
            jax.ShapeDtypeStruct((rows, 2 * HEAD_WIDTH), bf16),
            jax.ShapeDtypeStruct((rows, tok), bf16),
        ),
        in_specs=[VMEM] * 3,
        out_specs=(VMEM, VMEM),
        compiler_params=params,
        name="pack",
    )(row_route.reshape(1, tok), keys, values)
    got_kv = lax.all_to_all(packed_kv.reshape(n, SLOTS, 2 * HEAD_WIDTH), "ctx", 0, 0, tiled=True)
    packed_q = jnp.dot(pick, queries, preferred_element_type=jnp.float32).astype(bf16)
    got_q = lax.all_to_all(packed_q.reshape(n, SLOTS, width), "ctx", 0, 0, tiled=True)

    my_kv, my_pick = pl.pallas_call(
        functools.partial(unpack_kernel, n),
        out_shape=(
            jax.ShapeDtypeStruct((tok, 2 * HEAD_WIDTH), bf16),
            jax.ShapeDtypeStruct((tok, rows), bf16),
        ),
        in_specs=[VMEM],
        out_specs=(VMEM, VMEM),
        compiler_params=params,
        name="unpack",
    )(got_kv.reshape(rows, 2 * HEAD_WIDTH))

    pairs = [[2 * c, 2 * c + 1] for c in range(n // 2)]

    def both_cores(x):
        return lax.all_gather(x, "ctx", axis_index_groups=pairs, axis=0, tiled=True)

    own = both_cores(my_kv)
    far = []
    for t in range(4):
        route = [
            (2 * (chip - 2 * t - 1 - core) + core, 2 * chip + core)
            for chip in range(n // 2)
            for core in range(2)
            if chip - 2 * t - 1 - core >= 0
        ]
        far.append(both_cores(lax.ppermute(own, "ctx", route)))

    first, second = pl.pallas_call(
        functools.partial(attend_kernel, groups),
        out_shape=(
            jax.ShapeDtypeStruct((tok // 2, width), bf16),
            jax.ShapeDtypeStruct((tok // 2, width), bf16),
        ),
        in_specs=[SMEM, SMEM] + [VMEM] * 7,
        out_specs=(VMEM, VMEM),
        scratch_shapes=[pltpu.VMEM((groups * tok, HEAD_WIDTH), bf16)],
        compiler_params=params,
        name="attend",
    )(lengths, index.astype(jnp.int32).reshape(1), my_pick, got_q.reshape(rows, width), own, *far)

    h = n // 2
    first = lax.ppermute(first, "ctx", [(j, 2 * j if j < h else 2 * n - 1 - 2 * j) for j in range(n)])
    second = lax.ppermute(
        second, "ctx", [(j, 2 * j + 1 if j < h else 2 * n - 2 - 2 * j) for j in range(n)]
    )
    even = index % 2 == 0
    return jnp.concatenate(
        [jnp.where(even, first, second), jnp.where(even, second, first)], axis=0
    )


def solution(mesh):
    placed = (P("ctx", "tp"), P("ctx", "tp"), P("ctx", "tp"), P("ctx"), P())
    return jax.shard_map(
        local, mesh=mesh, in_specs=placed, out_specs=P("ctx", "tp"), check_vma=False
    )
```

```python
import functools
import math

import jax
import jax.numpy as jnp
from jax import lax
from jax.experimental import pallas as pl
from jax.experimental.pallas import tpu as pltpu
from jax.sharding import PartitionSpec as P

HEAD_WIDTH = 128
SLOTS = 8
CAP = 6
PLANE = 8
STEPS = 4
NEG = -1e30
VMEM = pl.BlockSpec(memory_space=pltpu.VMEM)
ANY = pl.BlockSpec(memory_space=pl.ANY)
SMEM = pl.BlockSpec(memory_space=pltpu.SMEM)


def iota(shape, dim):
    return lax.broadcasted_iota(jnp.int32, shape, dim)


def divide(x, by):
    return ((x.astype(jnp.float32) + 0.5) * (1.0 / by)).astype(jnp.int32)


def hot(mask):
    return jnp.where(mask, jnp.float32(1), jnp.float32(0)).astype(jnp.bfloat16)


def times(a, b):
    return jnp.dot(a, b, preferred_element_type=jnp.float32)


def times_t(a, b):
    return lax.dot_general(a, b, (((1,), (1,)), ((), ())), preferred_element_type=jnp.float32)


def pack_kernel(n, route_hbm, q_hbm, k_hbm, v_hbm, out_ref, route_ref, q_ref, k_ref, v_ref, sems):
    copies = [
        pltpu.make_async_copy(src, dst, sems.at[i])
        for i, (src, dst) in enumerate(
            ((route_hbm, route_ref), (k_hbm, k_ref), (v_hbm, v_ref), (q_hbm, q_ref))
        )
    ]
    for copy in copies:
        copy.start()
    tok, width = q_ref.shape
    rows = n * SLOTS
    copies[0].wait()
    route = route_ref[...]
    owner = divide(route, tok)
    slot = route - owner * tok
    square = (tok, tok)
    down, across = iota(square, 0), iota(square, 1)
    along = jnp.broadcast_to(owner, square)
    column = jnp.sum(jnp.where(down == across, along, 0), axis=1, keepdims=True)
    order = jnp.sum(
        jnp.where((column == along) & (down < across), 1, 0), axis=0, keepdims=True
    )
    wide = (rows, tok)
    line = iota(wide, 0)
    to = owner * SLOTS

    def pick(row, valid=None):
        where_to = to + row
        if valid is not None:
            where_to = jnp.where(valid, where_to, -1)
        return hot(line == jnp.broadcast_to(where_to, wide))

    value_picks = {
        group: pick(CAP + order - first, (order >= first) & (order < first + 2))
        for group, first in ((4, 0), (0, 2), (1, 4))
    }
    lanes = (HEAD_WIDTH, tok)
    places = jnp.where(
        iota(lanes, 0) == jnp.broadcast_to(order, lanes),
        jnp.broadcast_to(slot + 1, lanes).astype(jnp.float32),
        jnp.float32(0),
    ).astype(jnp.bfloat16)
    extra = {2: times_t(pick(CAP), places)}
    main = pick(order)
    copies[1].wait()
    copies[2].wait()
    for group, chosen in value_picks.items():
        extra[group] = times(chosen, v_ref[...])
    extra[4] += times(main, k_ref[...])
    copies[3].wait()
    packed = times(main, q_ref[...])
    for group in range(5):
        part = slice(group * HEAD_WIDTH, (group + 1) * HEAD_WIDTH)
        value = extra.get(group)
        if group < 4:
            value = packed[:, part] if value is None else packed[:, part] + value
        out_ref[:, part] = value.astype(jnp.bfloat16)


def unpack_kernel(n, keys, index_ref, got_ref, *outs):
    rows = n * SLOTS
    tall = (n, rows)
    mark_row = iota(tall, 0) * SLOTS + CAP

    def group(i):
        return got_ref[:, i * HEAD_WIDTH : (i + 1) * HEAD_WIDTH]

    marks = times(hot(iota(tall, 1) == mark_row), group(2)).astype(jnp.bfloat16)
    mine = iota(tall, 1) - iota(tall, 0) * SLOTS
    mine = (mine >= 0) & (mine < SLOTS)
    lanes = (HEAD_WIDTH, rows)
    row = iota(lanes, 1) & (SLOTS - 1)

    def place_of(lane):
        spread = times(marks, hot(iota(lanes, 0) == lane))
        return jnp.sum(jnp.where(mine, spread, jnp.float32(0)), axis=0, keepdims=True)

    def pick(place, count, offset):
        wide = (count, rows)
        want = (iota(wide, 0) + 1 + offset).astype(jnp.float32)
        return hot(want == jnp.broadcast_to(place, wide))

    main = place_of(jnp.where(row < CAP, row, -1))
    if keys:
        (kv_ref,) = outs
        tok = kv_ref.shape[0]
        kv_ref[:, :HEAD_WIDTH] = times(pick(main, tok, 0), group(4)).astype(jnp.bfloat16)
        v = sum(
            times(pick(place_of(jnp.where(row >= CAP, row - CAP + first, -1)), tok, 0), group(at))
            for at, first in ((4, 0), (0, 2), (1, 4))
        )
        kv_ref[:, HEAD_WIDTH:] = v.astype(jnp.bfloat16)
        return
    half, width = outs[0].shape
    even = index_ref[0] % 2 == 0
    for ref, own in zip(outs, (even, jnp.logical_not(even))):
        chosen = pick(main, half, jnp.where(own, 0, half))
        ref[...] = times(chosen, got_ref[:, :width]).astype(jnp.bfloat16)


def attend_kernel(n, groups, lengths_ref, index_ref, q1_ref, q2_ref, *rest):
    key_refs, value_refs = rest[:STEPS], rest[STEPS : 2 * STEPS]
    heads_ref, top_ref, acc_ref, scores_ref = rest[2 * STEPS :]
    half = q1_ref.shape[0]
    tok = 2 * half
    span = key_refs[0].shape[0]
    index = index_ref[0]
    even = index % 2 == 0
    chunk = jnp.where(even, index // 2, n - 1 - index // 2)
    first_row = chunk * tok
    run = first_row // span
    scale = HEAD_WIDTH ** (-0.5) * math.log2(math.e)

    for g in range(groups):
        lanes = slice(g * HEAD_WIDTH, (g + 1) * HEAD_WIDTH)
        for ref, at in ((q1_ref, g * tok), (q2_ref, g * tok + half)):
            scaled = ref[:, lanes].astype(jnp.float32) * scale
            upper = scaled.astype(jnp.bfloat16)
            lower = (scaled - upper.astype(jnp.float32)).astype(jnp.bfloat16)
            heads_ref[at : at + half, :HEAD_WIDTH] = upper
            heads_ref[at : at + half, HEAD_WIDTH:] = lower

    column = (tok, HEAD_WIDTH)
    query_pos = first_row + iota(column, 0)
    start = jnp.zeros(column, jnp.int32)
    first_start = last_start = end = jnp.int32(0)
    for i in range(lengths_ref.shape[0]):
        end = end + lengths_ref[i]
        start = jnp.where(query_pos >= end, end, start)
        first_start = jnp.where(first_row >= end, end, first_start)
        last_start = jnp.where(first_row + tok - 1 >= end, end, last_start)

    def score(step, base, masked):
        k = key_refs[step][...]
        k = jnp.concatenate([k, k], axis=1)
        own = step == 0
        reach = span // HEAD_WIDTH
        if masked:
            key_pos = base + iota((tok, span), 1)
            allowed = key_pos >= jnp.concatenate([start] * reach, axis=1)
            if own:
                allowed &= key_pos <= jnp.concatenate([query_pos] * reach, axis=1)
        for g in range(groups):
            rows = slice(g * tok, (g + 1) * tok)
            s = times_t(heads_ref[rows, :], k)
            if masked:
                s = jnp.where(allowed, s, NEG)
            scores_ref[rows, step * span : (step + 1) * span] = s
            top = s[:, :HEAD_WIDTH]
            for i in range(1, reach):
                top = jnp.maximum(top, s[:, i * HEAD_WIDTH : (i + 1) * HEAD_WIDTH])
            if not own:
                top = jnp.maximum(top, top_ref[rows, :])
            top_ref[rows, :] = top

    def weigh(step):
        v = value_refs[step][...]
        v = jnp.concatenate([v, jnp.ones_like(v)], axis=1)
        for g in range(groups):
            rows = slice(g * tok, (g + 1) * tok)
            top = jnp.concatenate([top_ref[rows, :]] * (span // HEAD_WIDTH), axis=1)
            w = jnp.exp2(scores_ref[rows, step * span : (step + 1) * span] - top)
            acc = times(w.astype(jnp.bfloat16), v)
            if step:
                acc += acc_ref[rows, :]
            acc_ref[rows, :] = acc

    bases = [(run - step) * span for step in range(STEPS)]

    def needed(step):
        return (bases[step] >= 0) & (bases[step] + span > first_start)

    score(0, bases[0], True)
    for step in range(1, STEPS):
        clear = bases[step] >= last_start

        @pl.when(needed(step) & clear)
        def _(step=step):
            score(step, bases[step], False)

        @pl.when(needed(step) & jnp.logical_not(clear))
        def _(step=step):
            score(step, bases[step], True)

    for g in range(groups):
        rows = slice(g * tok, (g + 1) * tok)
        top = jnp.max(top_ref[rows, :], axis=1, keepdims=True)
        top_ref[rows, :] = jnp.broadcast_to(top, column)

    weigh(0)
    for step in range(1, STEPS):

        @pl.when(needed(step))
        def _(step=step):
            weigh(step)


def finish_kernel(
    n, groups, lengths_ref, index_ref, heads_ref, top_ref, acc_ref, key_ref, value_ref, first_ref, second_ref
):
    tok = heads_ref.shape[0] // groups
    half = tok // 2
    span = key_ref.shape[0]
    reach = span // HEAD_WIDTH
    index = index_ref[0]
    chunk = jnp.where(index % 2 == 0, index // 2, n - 1 - index // 2)
    first_row = chunk * tok
    base = (first_row // span - STEPS) * span
    column = (tok, HEAD_WIDTH)
    start = jnp.zeros(column, jnp.int32)
    first_start = end = jnp.int32(0)
    for i in range(lengths_ref.shape[0]):
        end = end + lengths_ref[i]
        start = jnp.where(first_row + iota(column, 0) >= end, end, start)
        first_start = jnp.where(first_row >= end, end, first_start)

    def write(g, acc):
        lanes = slice(g * HEAD_WIDTH, (g + 1) * HEAD_WIDTH)
        out = (acc[:, :HEAD_WIDTH] / acc[:, HEAD_WIDTH:]).astype(jnp.bfloat16)
        first_ref[:, lanes] = out[:half]
        second_ref[:, lanes] = out[half:]

    needed = (base >= 0) & (base + span > first_start)

    @pl.when(needed)
    def _():
        k, v = key_ref[...], value_ref[...]
        k = jnp.concatenate([k, k], axis=1)
        v = jnp.concatenate([v, jnp.ones_like(v)], axis=1)
        key_pos = base + iota((tok, span), 1)
        allowed = key_pos >= jnp.concatenate([start] * reach, axis=1)
        for g in range(groups):
            rows = slice(g * tok, (g + 1) * tok)
            s = jnp.where(allowed, times_t(heads_ref[rows, :], k), NEG)
            top = s[:, :HEAD_WIDTH]
            for i in range(1, reach):
                top = jnp.maximum(top, s[:, i * HEAD_WIDTH : (i + 1) * HEAD_WIDTH])
            top = jnp.broadcast_to(jnp.max(top, axis=1, keepdims=True), column)
            before = top_ref[rows, :]
            top = jnp.maximum(top, before)
            w = jnp.exp2(s - jnp.concatenate([top] * reach, axis=1)).astype(jnp.bfloat16)
            keep = jnp.exp2(before - top)
            write(g, times(w, v) + acc_ref[rows, :] * jnp.concatenate([keep, keep], axis=1))

    @pl.when(jnp.logical_not(needed))
    def _():
        for g in range(groups):
            write(g, acc_ref[g * tok : (g + 1) * tok, :])


def local(queries, keys, values, row_route, lengths):
    n = lax.axis_size("ctx")
    index = lax.axis_index("ctx")
    tok, width = queries.shape
    half = tok // 2
    groups = width // HEAD_WIDTH
    rows = n * SLOTS
    lanes = width + HEAD_WIDTH
    bf16 = jnp.bfloat16
    here = index.astype(jnp.int32).reshape(1)
    even = index % 2 == 0

    packed = pl.pallas_call(
        functools.partial(pack_kernel, n),
        out_shape=jax.ShapeDtypeStruct((rows, lanes), bf16),
        in_specs=[ANY] * 4,
        out_specs=VMEM,
        scratch_shapes=[
            pltpu.VMEM((1, tok), jnp.int32),
            pltpu.VMEM((tok, width), bf16),
            pltpu.VMEM((tok, HEAD_WIDTH), bf16),
            pltpu.VMEM((tok, HEAD_WIDTH), bf16),
            pltpu.SemaphoreType.DMA((4,)),
        ],
        compiler_params=pltpu.CompilerParams(vmem_limit_bytes=60 * 2**20),
        name="pack",
    )(row_route.reshape(1, tok), queries, keys, values)
    got = lax.all_to_all(packed.reshape(n, SLOTS, lanes), "ctx", 0, 0, tiled=True)

    params = pltpu.CompilerParams(vmem_limit_bytes=48 * 2**20)
    part = jax.ShapeDtypeStruct((half, width), bf16)
    got = got.reshape(rows, lanes)

    def unpack(keys, *shapes):
        return pl.pallas_call(
            functools.partial(unpack_kernel, n, keys),
            out_shape=shapes,
            in_specs=[SMEM, VMEM],
            out_specs=(VMEM,) * len(shapes),
            compiler_params=params,
            name="unpack_kv" if keys else "unpack_q",
        )(here, got)

    (my_kv,) = unpack(True, jax.ShapeDtypeStruct((tok, 2 * HEAD_WIDTH), bf16))
    keep, give = unpack(False, part, part)

    planes = n // PLANE
    groups_of = [list(range(z * PLANE, (z + 1) * PLANE)) for z in range(planes)]
    plane = lax.all_gather(my_kv, "ctx", axis_index_groups=groups_of, axis=0, tiled=True)
    plane = plane.reshape(PLANE, 2, half, 2 * HEAD_WIDTH)
    run = jnp.where(even, plane[:, 0], plane[::-1, 1]).reshape(PLANE * half, 2 * HEAD_WIDTH)
    run_keys, run_values = [run[:, :HEAD_WIDTH]], [run[:, HEAD_WIDTH:]]
    chain = []
    for chip in range(PLANE // 2):
        stops = [z * PLANE + 2 * chip for z in range(planes)]
        stops += [stop + 1 for stop in reversed(stops)]
        chain += list(zip(stops[:-1], stops[1:]))
    for step in range(STEPS):
        run_keys.append(lax.ppermute(run_keys[step], "ctx", chain))
        run_values.append(lax.ppermute(run_values[step], "ctx", chain))

    swap = [(i, i ^ 1) for i in range(n)]
    taken = lax.ppermute(give, "ctx", swap)
    sums = (
        jax.ShapeDtypeStruct((groups * tok, 2 * HEAD_WIDTH), bf16),
        jax.ShapeDtypeStruct((groups * tok, HEAD_WIDTH), jnp.float32),
        jax.ShapeDtypeStruct((groups * tok, 2 * HEAD_WIDTH), jnp.float32),
    )
    params = pltpu.CompilerParams(vmem_limit_bytes=32 * 2**20)
    pairs = groups * tok * PLANE * half
    state = pl.pallas_call(
        functools.partial(attend_kernel, n, groups),
        out_shape=sums,
        in_specs=[SMEM, SMEM] + [VMEM] * (2 * STEPS + 2),
        out_specs=(VMEM,) * 3,
        scratch_shapes=[pltpu.VMEM((groups * tok, STEPS * PLANE * half), jnp.float32)],
        compiler_params=params,
        cost_estimate=pl.CostEstimate(
            flops=64 * STEPS * HEAD_WIDTH * pairs,
            bytes_accessed=2**23,
            transcendentals=8 * STEPS * pairs,
        ),
        name="attend",
    )(lengths, here, keep, taken, *run_keys[:STEPS], *run_values[:STEPS])
    first, second = pl.pallas_call(
        functools.partial(finish_kernel, n, groups),
        out_shape=(part, part),
        in_specs=[SMEM, SMEM] + [VMEM] * 5,
        out_specs=(VMEM, VMEM),
        compiler_params=params,
        name="finish",
    )(lengths, here, *state, run_keys[STEPS], run_values[STEPS])

    second = lax.ppermute(second, "ctx", swap)
    return jnp.concatenate(
        [jnp.where(even, first, second), jnp.where(even, second, first)], axis=0
    )


def solution(mesh):
    placed = (P("ctx", "tp"), P("ctx", "tp"), P("ctx", "tp"), P("ctx"), P())
    return jax.shard_map(
        local, mesh=mesh, in_specs=placed, out_specs=P("ctx", "tp"), check_vma=False
    )
```

```python
import functools
import math

import jax
import jax.numpy as jnp
from jax import lax
from jax.experimental import pallas as pl
from jax.experimental.pallas import tpu as pltpu
from jax.sharding import PartitionSpec as P

HEAD_WIDTH = 128
SLOTS = 8
CAP = 6
PLANE = 8
STEPS = 4
NEG = -1e30
VMEM = pl.BlockSpec(memory_space=pltpu.VMEM)
ANY = pl.BlockSpec(memory_space=pl.ANY)
SMEM = pl.BlockSpec(memory_space=pltpu.SMEM)


def iota(shape, dim):
    return lax.broadcasted_iota(jnp.int32, shape, dim)


def divide(x, by):
    return ((x.astype(jnp.float32) + 0.5) * (1.0 / by)).astype(jnp.int32)


def hot(mask):
    return jnp.where(mask, jnp.float32(1), jnp.float32(0)).astype(jnp.bfloat16)


def times(a, b):
    return jnp.dot(a, b, preferred_element_type=jnp.float32)


def times_t(a, b):
    return lax.dot_general(a, b, (((1,), (1,)), ((), ())), preferred_element_type=jnp.float32)


def pack_kernel(n, route_hbm, q_hbm, k_hbm, v_hbm, out_ref, route_ref, q_ref, k_ref, v_ref, sems):
    copies = [
        pltpu.make_async_copy(src, dst, sems.at[i])
        for i, (src, dst) in enumerate(
            ((route_hbm, route_ref), (k_hbm, k_ref), (v_hbm, v_ref), (q_hbm, q_ref))
        )
    ]
    for copy in copies:
        copy.start()
    tok, width = q_ref.shape
    rows = n * SLOTS
    copies[0].wait()
    route = route_ref[...]
    owner = divide(route, tok)
    slot = route - owner * tok
    square = (tok, tok)
    down, across = iota(square, 0), iota(square, 1)
    along = jnp.broadcast_to(owner, square)
    column = jnp.sum(jnp.where(down == across, along, 0), axis=1, keepdims=True)
    order = jnp.sum(
        jnp.where((column == along) & (down < across), 1, 0), axis=0, keepdims=True
    )
    wide = (rows, tok)
    line = iota(wide, 0)
    to = owner * SLOTS

    def pick(row, valid=None):
        where_to = to + row
        if valid is not None:
            where_to = jnp.where(valid, where_to, -1)
        return hot(line == jnp.broadcast_to(where_to, wide))

    value_picks = {
        group: pick(CAP + order - first, (order >= first) & (order < first + 2))
        for group, first in ((4, 0), (0, 2), (1, 4))
    }
    lanes = (HEAD_WIDTH, tok)
    places = jnp.where(
        iota(lanes, 0) == jnp.broadcast_to(order, lanes),
        jnp.broadcast_to(slot + 1, lanes).astype(jnp.float32),
        jnp.float32(0),
    ).astype(jnp.bfloat16)
    extra = {2: times_t(pick(CAP), places)}
    main = pick(order)
    copies[1].wait()
    copies[2].wait()
    for group, chosen in value_picks.items():
        extra[group] = times(chosen, v_ref[...])
    extra[4] += times(main, k_ref[...])
    copies[3].wait()
    packed = times(main, q_ref[...])
    for group in range(5):
        part = slice(group * HEAD_WIDTH, (group + 1) * HEAD_WIDTH)
        value = extra.get(group)
        if group < 4:
            value = packed[:, part] if value is None else packed[:, part] + value
        out_ref[:, part] = value.astype(jnp.bfloat16)


def unpack_kernel(n, index_ref, got_ref, kv_ref, keep_ref, give_ref):
    rows = n * SLOTS
    tall = (n, rows)
    mark_row = iota(tall, 0) * SLOTS + CAP

    def group(i):
        return got_ref[:, i * HEAD_WIDTH : (i + 1) * HEAD_WIDTH]

    marks = times(hot(iota(tall, 1) == mark_row), group(2)).astype(jnp.bfloat16)
    mine = iota(tall, 1) - iota(tall, 0) * SLOTS
    mine = (mine >= 0) & (mine < SLOTS)
    lanes = (HEAD_WIDTH, rows)
    row = iota(lanes, 1) & (SLOTS - 1)

    def place_of(lane):
        spread = times(marks, hot(iota(lanes, 0) == lane))
        return jnp.sum(jnp.where(mine, spread, jnp.float32(0)), axis=0, keepdims=True)

    def pick(place, count, offset):
        wide = (count, rows)
        want = (iota(wide, 0) + 1 + offset).astype(jnp.float32)
        return hot(want == jnp.broadcast_to(place, wide))

    main = place_of(jnp.where(row < CAP, row, -1))
    tok = kv_ref.shape[0]
    kv_ref[:, :HEAD_WIDTH] = times(pick(main, tok, 0), group(4)).astype(jnp.bfloat16)
    v = sum(
        times(pick(place_of(jnp.where(row >= CAP, row - CAP + first, -1)), tok, 0), group(at))
        for at, first in ((4, 0), (0, 2), (1, 4))
    )
    kv_ref[:, HEAD_WIDTH:] = v.astype(jnp.bfloat16)
    half, width = keep_ref.shape
    even = index_ref[0] % 2 == 0
    for ref, own in ((keep_ref, even), (give_ref, jnp.logical_not(even))):
        chosen = pick(main, half, jnp.where(own, 0, half))
        ref[...] = times(chosen, got_ref[:, :width]).astype(jnp.bfloat16)


def attend_kernel(n, groups, steps, lengths_ref, index_ref, *refs):
    count = len(steps)
    begin = steps[0] == 0
    given = 2 if begin else 3
    key_refs = dict(zip(steps, refs[given : given + count]))
    value_refs = dict(zip(steps, refs[given + count : given + 2 * count]))
    if begin:
        q1_ref, q2_ref = refs[:given]
        heads_ref, top_ref, acc_ref, scores_ref = refs[given + 2 * count :]
    else:
        heads_ref, old_top_ref, old_acc_ref = refs[:given]
        top_ref, acc_ref, scores_ref = refs[given + 2 * count :]
    tok = heads_ref.shape[0] // groups
    half = tok // 2
    span = key_refs[steps[0]].shape[0]
    index = index_ref[0]
    chunk = jnp.where(index % 2 == 0, index // 2, n - 1 - index // 2)
    first_row = chunk * tok
    run = first_row // span

    if begin:
        scale = HEAD_WIDTH ** (-0.5) * math.log2(math.e)
        for g in range(groups):
            lanes = slice(g * HEAD_WIDTH, (g + 1) * HEAD_WIDTH)
            for ref, at in ((q1_ref, g * tok), (q2_ref, g * tok + half)):
                scaled = ref[:, lanes].astype(jnp.float32) * scale
                upper = scaled.astype(jnp.bfloat16)
                lower = (scaled - upper.astype(jnp.float32)).astype(jnp.bfloat16)
                heads_ref[at : at + half, :HEAD_WIDTH] = upper
                heads_ref[at : at + half, HEAD_WIDTH:] = lower
    else:
        top_ref[...] = old_top_ref[...]

    column = (tok, HEAD_WIDTH)
    query_pos = first_row + iota(column, 0)
    start = jnp.zeros(column, jnp.int32)
    first_start = last_start = end = jnp.int32(0)
    for i in range(lengths_ref.shape[0]):
        end = end + lengths_ref[i]
        start = jnp.where(query_pos >= end, end, start)
        first_start = jnp.where(first_row >= end, end, first_start)
        last_start = jnp.where(first_row + tok - 1 >= end, end, last_start)

    def score(step, base, masked):
        k = key_refs[step][...]
        k = jnp.concatenate([k, k], axis=1)
        reach = span // HEAD_WIDTH
        if masked:
            key_pos = base + iota((tok, span), 1)
            allowed = key_pos >= jnp.concatenate([start] * reach, axis=1)
            if step == 0:
                allowed &= key_pos <= jnp.concatenate([query_pos] * reach, axis=1)
        for t0 in range(0, span, 256):
            s = times_t(heads_ref[...], k[t0 : t0 + 256, :])
            if masked:
                part = allowed[:, t0 : t0 + 256]
                s = jnp.where(jnp.concatenate([part] * groups, axis=0), s, NEG)
            at = (step - steps[0]) * span + t0
            scores_ref[:, at : at + 256] = s
            top = jnp.maximum(s[:, :HEAD_WIDTH], s[:, HEAD_WIDTH:])
            if step or t0:
                top = jnp.maximum(top, top_ref[...])
            top_ref[...] = top

    def weigh(step):
        v = value_refs[step][...]
        v = jnp.concatenate([v, jnp.ones_like(v)], axis=1)
        at = (step - steps[0]) * span
        for r0 in range(0, groups * tok, 2 * tok):
            rows = slice(r0, r0 + 2 * tok)
            top = jnp.concatenate([top_ref[rows, :]] * (span // HEAD_WIDTH), axis=1)
            w = jnp.exp2(scores_ref[rows, at : at + span] - top)
            acc = times(w.astype(jnp.bfloat16), v)
            if step:
                acc += acc_ref[rows, :]
            acc_ref[rows, :] = acc

    def base_of(step):
        return (run - step) * span

    def needed(step):
        return (base_of(step) >= 0) & (base_of(step) + span > first_start)

    for step in steps:
        if step == 0:
            score(0, base_of(0), True)
            continue
        clear = base_of(step) >= last_start

        @pl.when(needed(step) & clear)
        def _(step=step):
            score(step, base_of(step), False)

        @pl.when(needed(step) & jnp.logical_not(clear))
        def _(step=step):
            score(step, base_of(step), True)

    def settle():
        for g in range(groups):
            rows = slice(g * tok, (g + 1) * tok)
            top = jnp.max(top_ref[rows, :], axis=1, keepdims=True)
            top = jnp.broadcast_to(top, column)
            top_ref[rows, :] = top
            if not begin:
                keep = jnp.exp2(old_top_ref[rows, :] - top)
                acc_ref[rows, :] = old_acc_ref[rows, :] * jnp.concatenate([keep, keep], axis=1)

    if begin:
        settle()
    else:
        pl.when(needed(steps[0]))(settle)

        @pl.when(jnp.logical_not(needed(steps[0])))
        def _():
            acc_ref[...] = old_acc_ref[...]

    for step in steps:
        if step == 0:
            weigh(0)
        else:

            @pl.when(needed(step))
            def _(step=step):
                weigh(step)


def finish_kernel(
    n, groups, lengths_ref, index_ref, heads_ref, top_ref, acc_ref, key_ref, value_ref, first_ref, second_ref
):
    tok = heads_ref.shape[0] // groups
    half = tok // 2
    span = key_ref.shape[0]
    reach = span // HEAD_WIDTH
    index = index_ref[0]
    chunk = jnp.where(index % 2 == 0, index // 2, n - 1 - index // 2)
    first_row = chunk * tok
    base = (first_row // span - STEPS) * span
    column = (tok, HEAD_WIDTH)
    start = jnp.zeros(column, jnp.int32)
    first_start = end = jnp.int32(0)
    for i in range(lengths_ref.shape[0]):
        end = end + lengths_ref[i]
        start = jnp.where(first_row + iota(column, 0) >= end, end, start)
        first_start = jnp.where(first_row >= end, end, first_start)

    def write(g, acc):
        lanes = slice(g * HEAD_WIDTH, (g + 1) * HEAD_WIDTH)
        out = (acc[:, :HEAD_WIDTH] / acc[:, HEAD_WIDTH:]).astype(jnp.bfloat16)
        first_ref[:, lanes] = out[:half]
        second_ref[:, lanes] = out[half:]

    needed = (base >= 0) & (base + span > first_start)

    @pl.when(needed)
    def _():
        k, v = key_ref[...], value_ref[...]
        k = jnp.concatenate([k, k], axis=1)
        v = jnp.concatenate([v, jnp.ones_like(v)], axis=1)
        key_pos = base + iota((tok, span), 1)
        allowed = key_pos >= jnp.concatenate([start] * reach, axis=1)
        for g in range(groups):
            rows = slice(g * tok, (g + 1) * tok)
            s = jnp.where(allowed, times_t(heads_ref[rows, :], k), NEG)
            top = s[:, :HEAD_WIDTH]
            for i in range(1, reach):
                top = jnp.maximum(top, s[:, i * HEAD_WIDTH : (i + 1) * HEAD_WIDTH])
            top = jnp.broadcast_to(jnp.max(top, axis=1, keepdims=True), column)
            before = top_ref[rows, :]
            top = jnp.maximum(top, before)
            w = jnp.exp2(s - jnp.concatenate([top] * reach, axis=1)).astype(jnp.bfloat16)
            keep = jnp.exp2(before - top)
            write(g, times(w, v) + acc_ref[rows, :] * jnp.concatenate([keep, keep], axis=1))

    @pl.when(jnp.logical_not(needed))
    def _():
        for g in range(groups):
            write(g, acc_ref[g * tok : (g + 1) * tok, :])


def local(queries, keys, values, row_route, lengths):
    n = lax.axis_size("ctx")
    index = lax.axis_index("ctx")
    tok, width = queries.shape
    half = tok // 2
    groups = width // HEAD_WIDTH
    rows = n * SLOTS
    lanes = width + HEAD_WIDTH
    bf16 = jnp.bfloat16
    here = index.astype(jnp.int32).reshape(1)
    even = index % 2 == 0

    packed = pl.pallas_call(
        functools.partial(pack_kernel, n),
        out_shape=jax.ShapeDtypeStruct((rows, lanes), bf16),
        in_specs=[ANY] * 4,
        out_specs=VMEM,
        scratch_shapes=[
            pltpu.VMEM((1, tok), jnp.int32),
            pltpu.VMEM((tok, width), bf16),
            pltpu.VMEM((tok, HEAD_WIDTH), bf16),
            pltpu.VMEM((tok, HEAD_WIDTH), bf16),
            pltpu.SemaphoreType.DMA((4,)),
        ],
        compiler_params=pltpu.CompilerParams(vmem_limit_bytes=60 * 2**20),
        name="pack",
    )(row_route.reshape(1, tok), queries, keys, values)
    got = lax.all_to_all(packed.reshape(n, SLOTS, lanes), "ctx", 0, 0, tiled=True)

    params = pltpu.CompilerParams(vmem_limit_bytes=48 * 2**20)
    part = jax.ShapeDtypeStruct((half, width), bf16)
    my_kv, keep, give = pl.pallas_call(
        functools.partial(unpack_kernel, n),
        out_shape=(jax.ShapeDtypeStruct((tok, 2 * HEAD_WIDTH), bf16), part, part),
        in_specs=[SMEM, VMEM],
        out_specs=(VMEM, VMEM, VMEM),
        compiler_params=params,
        name="unpack",
    )(here, got.reshape(rows, lanes))

    planes = n // PLANE
    groups_of = [list(range(z * PLANE, (z + 1) * PLANE)) for z in range(planes)]
    plane = lax.all_gather(my_kv, "ctx", axis_index_groups=groups_of, axis=0, tiled=True)
    plane = plane.reshape(PLANE, 2, half, 2 * HEAD_WIDTH)
    run = jnp.where(even, plane[:, 0], plane[::-1, 1]).reshape(PLANE * half, 2 * HEAD_WIDTH)
    run_keys, run_values = [run[:, :HEAD_WIDTH]], [run[:, HEAD_WIDTH:]]
    chain = []
    for chip in range(PLANE // 2):
        stops = [z * PLANE + 2 * chip for z in range(planes)]
        stops += [stop + 1 for stop in reversed(stops)]
        chain += list(zip(stops[:-1], stops[1:]))
    for step in range(STEPS):
        run_keys.append(lax.ppermute(run_keys[step], "ctx", chain))
        run_values.append(lax.ppermute(run_values[step], "ctx", chain))

    swap = [(i, i ^ 1) for i in range(n)]
    taken = lax.ppermute(give, "ctx", swap)
    scaled = jax.ShapeDtypeStruct((groups * tok, 2 * HEAD_WIDTH), bf16)
    sums = (
        jax.ShapeDtypeStruct((groups * tok, HEAD_WIDTH), jnp.float32),
        jax.ShapeDtypeStruct((groups * tok, 2 * HEAD_WIDTH), jnp.float32),
    )
    params = pltpu.CompilerParams(vmem_limit_bytes=32 * 2**20)
    pairs = groups * tok * PLANE * half

    def attend(steps, *arrays):
        arrays += tuple(run_keys[step] for step in steps)
        arrays += tuple(run_values[step] for step in steps)
        out = (scaled, *sums) if steps[0] == 0 else sums
        return pl.pallas_call(
            functools.partial(attend_kernel, n, groups, steps),
            out_shape=out,
            in_specs=[SMEM, SMEM] + [VMEM] * len(arrays),
            out_specs=(VMEM,) * len(out),
            scratch_shapes=[pltpu.VMEM((groups * tok, len(steps) * PLANE * half), jnp.float32)],
            compiler_params=params,
            cost_estimate=pl.CostEstimate(
                flops=64 * len(steps) * HEAD_WIDTH * pairs,
                bytes_accessed=2**23,
                transcendentals=8 * len(steps) * pairs,
            ),
            name=f"attend{steps[0]}",
        )(lengths, here, *arrays)

    heads, *state = attend((0,), keep, taken)
    state = (heads, *attend(tuple(range(1, STEPS)), heads, *state))
    first, second = pl.pallas_call(
        functools.partial(finish_kernel, n, groups),
        out_shape=(part, part),
        in_specs=[SMEM, SMEM] + [VMEM] * 5,
        out_specs=(VMEM, VMEM),
        compiler_params=params,
        name="finish",
    )(lengths, here, *state, run_keys[STEPS], run_values[STEPS])

    others = lax.all_gather(
        second, "ctx", axis_index_groups=[[i, i + 1] for i in range(0, n, 2)], axis=0
    )
    return jnp.where(
        even,
        jnp.concatenate([first, others[1]], axis=0),
        jnp.concatenate([others[0], first], axis=0),
    )


def solution(mesh):
    placed = (P("ctx", "tp"), P("ctx", "tp"), P("ctx", "tp"), P("ctx"), P())
    return jax.shard_map(
        local, mesh=mesh, in_specs=placed, out_specs=P("ctx", "tp"), check_vma=False
    )
```

```python
import functools
import math

import jax
import jax.numpy as jnp
from jax import lax
from jax.experimental import pallas as pl
from jax.experimental.pallas import tpu as pltpu
from jax.sharding import PartitionSpec as P

HEAD_WIDTH = 128
SLOTS = 8
CAP = 6
PLANE = 8
STEPS = 4
NEG = -1e30
VMEM = pl.BlockSpec(memory_space=pltpu.VMEM)
ANY = pl.BlockSpec(memory_space=pl.ANY)
SMEM = pl.BlockSpec(memory_space=pltpu.SMEM)


def iota(shape, dim):
    return lax.broadcasted_iota(jnp.int32, shape, dim)


def divide(x, by):
    return ((x.astype(jnp.float32) + 0.5) * (1.0 / by)).astype(jnp.int32)


def hot(mask):
    return jnp.where(mask, jnp.float32(1), jnp.float32(0)).astype(jnp.bfloat16)


def times(a, b):
    return jnp.dot(a, b, preferred_element_type=jnp.float32)


def times_t(a, b):
    return lax.dot_general(a, b, (((1,), (1,)), ((), ())), preferred_element_type=jnp.float32)


def pack_kernel(n, route_hbm, q_hbm, k_hbm, v_hbm, out_ref, route_ref, q_ref, k_ref, v_ref, sems):
    copies = [
        pltpu.make_async_copy(src, dst, sems.at[i])
        for i, (src, dst) in enumerate(
            ((route_hbm, route_ref), (k_hbm, k_ref), (v_hbm, v_ref), (q_hbm, q_ref))
        )
    ]
    for copy in copies:
        copy.start()
    tok, width = q_ref.shape
    rows = n * SLOTS
    copies[0].wait()
    route = route_ref[...]
    owner = divide(route, tok)
    slot = route - owner * tok
    square = (tok, tok)
    down, across = iota(square, 0), iota(square, 1)
    route_col = jnp.sum(
        jnp.where(down == across, jnp.broadcast_to(route, square), 0), axis=1, keepdims=True
    )
    owner_col = divide(route_col, tok)
    same = owner_col == jnp.broadcast_to(owner, square)
    order = jnp.sum(jnp.where(same & (down < across), 1, 0), axis=0, keepdims=True)
    order_col = jnp.sum(jnp.where(same & (across < down), 1, 0), axis=1, keepdims=True)
    wide = (rows, tok)
    line = iota(wide, 0)

    def pick(row):
        return hot(line == jnp.broadcast_to(owner * SLOTS + row, wide))

    spare = pick(CAP + (order & 1))
    column = (tok, HEAD_WIDTH)
    order_wide = jnp.broadcast_to(order_col, column)
    place = jnp.where(
        iota(column, 1) == order_wide, (route_col - owner_col * tok + 1).astype(jnp.float32), 0.0
    )
    main = pick(order)
    copies[1].wait()
    copies[2].wait()
    v = v_ref[...].astype(jnp.float32)
    pieces = [jnp.where((order_wide >> 1) == i, v, 0.0) for i in range(3)] + [place]
    extra = times(spare, jnp.concatenate(pieces, axis=1).astype(jnp.bfloat16))
    extra = {
        group: extra[:, i * HEAD_WIDTH : (i + 1) * HEAD_WIDTH]
        for i, group in enumerate((4, 0, 1, 2))
    }
    extra[4] += times(main, k_ref[...])
    copies[3].wait()
    packed = times(main, q_ref[...])
    for group in range(5):
        part = slice(group * HEAD_WIDTH, (group + 1) * HEAD_WIDTH)
        value = extra.get(group)
        if group < 4:
            value = packed[:, part] if value is None else packed[:, part] + value
        out_ref[:, part] = value.astype(jnp.bfloat16)


def unpack_kernel(n, index_ref, got_ref, kv_ref, keep_ref, give_ref):
    rows = n * SLOTS
    tall = (n, rows)
    mark_row = iota(tall, 0) * SLOTS + CAP

    def group(i):
        return got_ref[:, i * HEAD_WIDTH : (i + 1) * HEAD_WIDTH]

    marked = (iota(tall, 1) == mark_row) | (iota(tall, 1) == mark_row + 1)
    marks = times(hot(marked), group(2)).astype(jnp.bfloat16)
    mine = iota(tall, 1) - iota(tall, 0) * SLOTS
    mine = (mine >= 0) & (mine < SLOTS)
    lanes = (HEAD_WIDTH, rows)
    row = iota(lanes, 1) & (SLOTS - 1)

    def place_of(lane):
        spread = times(marks, hot(iota(lanes, 0) == lane))
        return jnp.sum(jnp.where(mine, spread, jnp.float32(0)), axis=0, keepdims=True)

    def pick(place, count, offset):
        wide = (count, rows)
        want = (iota(wide, 0) + 1 + offset).astype(jnp.float32)
        return hot(want == jnp.broadcast_to(place, wide))

    main = place_of(jnp.where(row < CAP, row, -1))
    tok = kv_ref.shape[0]
    kv_ref[:, :HEAD_WIDTH] = times(pick(main, tok, 0), group(4)).astype(jnp.bfloat16)
    v = sum(
        times(pick(place_of(jnp.where(row >= CAP, row - CAP + first, -1)), tok, 0), group(at))
        for at, first in ((4, 0), (0, 2), (1, 4))
    )
    kv_ref[:, HEAD_WIDTH:] = v.astype(jnp.bfloat16)
    half, width = keep_ref.shape
    even = index_ref[0] % 2 == 0
    for ref, own in ((keep_ref, even), (give_ref, jnp.logical_not(even))):
        chosen = pick(main, half, jnp.where(own, 0, half))
        ref[...] = times(chosen, got_ref[:, :width]).astype(jnp.bfloat16)


def attend_kernel(n, groups, steps, lengths_ref, index_ref, *refs):
    count = len(steps)
    begin = steps[0] == 0
    given = 2 if begin else 3
    key_refs = dict(zip(steps, refs[given : given + count]))
    value_refs = dict(zip(steps, refs[given + count : given + 2 * count]))
    if begin:
        q1_ref, q2_ref = refs[:given]
        heads_ref, top_ref, acc_ref, scores_ref = refs[given + 2 * count :]
    else:
        heads_ref, old_top_ref, old_acc_ref = refs[:given]
        top_ref, acc_ref, scores_ref = refs[given + 2 * count :]
    tok = heads_ref.shape[0] // groups
    half = tok // 2
    span = key_refs[steps[0]].shape[0]
    index = index_ref[0]
    chunk = jnp.where(index % 2 == 0, index // 2, n - 1 - index // 2)
    first_row = chunk * tok
    run = first_row // span

    if begin:
        scale = HEAD_WIDTH ** (-0.5) * math.log2(math.e)
        for g in range(groups):
            lanes = slice(g * HEAD_WIDTH, (g + 1) * HEAD_WIDTH)
            for ref, at in ((q1_ref, g * tok), (q2_ref, g * tok + half)):
                scaled = ref[:, lanes].astype(jnp.float32) * scale
                upper = scaled.astype(jnp.bfloat16)
                lower = (scaled - upper.astype(jnp.float32)).astype(jnp.bfloat16)
                heads_ref[at : at + half, :HEAD_WIDTH] = upper
                heads_ref[at : at + half, HEAD_WIDTH:] = lower
    else:
        top_ref[...] = old_top_ref[...]

    column = (tok, HEAD_WIDTH)
    query_pos = first_row + iota(column, 0)
    start = jnp.zeros(column, jnp.int32)
    first_start = last_start = end = jnp.int32(0)
    for i in range(lengths_ref.shape[0]):
        end = end + lengths_ref[i]
        start = jnp.where(query_pos >= end, end, start)
        first_start = jnp.where(first_row >= end, end, first_start)
        last_start = jnp.where(first_row + tok - 1 >= end, end, last_start)

    def score(step, base, masked):
        k = key_refs[step][...]
        k = jnp.concatenate([k, k], axis=1)
        reach = span // HEAD_WIDTH
        if masked:
            key_pos = base + iota((tok, span), 1)
            allowed = key_pos >= jnp.concatenate([start] * reach, axis=1)
            if step == 0:
                allowed &= key_pos <= jnp.concatenate([query_pos] * reach, axis=1)
        for t0 in range(0, span, 256):
            s = times_t(heads_ref[...], k[t0 : t0 + 256, :])
            if masked:
                part = allowed[:, t0 : t0 + 256]
                s = jnp.where(jnp.concatenate([part] * groups, axis=0), s, NEG)
            at = (step - steps[0]) * span + t0
            scores_ref[:, at : at + 256] = s
            top = jnp.maximum(s[:, :HEAD_WIDTH], s[:, HEAD_WIDTH:])
            if step or t0:
                top = jnp.maximum(top, top_ref[...])
            top_ref[...] = top

    def weigh(step):
        v = value_refs[step][...]
        v = jnp.concatenate([v, jnp.ones_like(v)], axis=1)
        at = (step - steps[0]) * span
        for r0 in range(0, groups * tok, 2 * tok):
            rows = slice(r0, r0 + 2 * tok)
            top = jnp.concatenate([top_ref[rows, :]] * (span // HEAD_WIDTH), axis=1)
            w = jnp.exp2(scores_ref[rows, at : at + span] - top)
            acc = times(w.astype(jnp.bfloat16), v)
            if step:
                acc += acc_ref[rows, :]
            acc_ref[rows, :] = acc

    def base_of(step):
        return (run - step) * span

    def needed(step):
        return (base_of(step) >= 0) & (base_of(step) + span > first_start)

    for step in steps:
        if step == 0:
            score(0, base_of(0), True)
            continue
        clear = base_of(step) >= last_start

        @pl.when(needed(step) & clear)
        def _(step=step):
            score(step, base_of(step), False)

        @pl.when(needed(step) & jnp.logical_not(clear))
        def _(step=step):
            score(step, base_of(step), True)

    def settle():
        for g in range(groups):
            rows = slice(g * tok, (g + 1) * tok)
            top = jnp.max(top_ref[rows, :], axis=1, keepdims=True)
            top = jnp.broadcast_to(top, column)
            top_ref[rows, :] = top
            if not begin:
                keep = jnp.exp2(old_top_ref[rows, :] - top)
                acc_ref[rows, :] = old_acc_ref[rows, :] * jnp.concatenate([keep, keep], axis=1)

    if begin:
        settle()
    else:
        pl.when(needed(steps[0]))(settle)

        @pl.when(jnp.logical_not(needed(steps[0])))
        def _():
            acc_ref[...] = old_acc_ref[...]

    for step in steps:
        if step == 0:
            weigh(0)
        else:

            @pl.when(needed(step))
            def _(step=step):
                weigh(step)


def finish_kernel(
    n, groups, lengths_ref, index_ref, heads_ref, top_ref, acc_ref, key_ref, value_ref, first_ref, second_ref, scores_ref, new_top_ref
):
    tok = heads_ref.shape[0] // groups
    half = tok // 2
    span = key_ref.shape[0]
    reach = span // HEAD_WIDTH
    index = index_ref[0]
    chunk = jnp.where(index % 2 == 0, index // 2, n - 1 - index // 2)
    first_row = chunk * tok
    base = (first_row // span - STEPS) * span
    column = (tok, HEAD_WIDTH)
    start = jnp.zeros(column, jnp.int32)
    first_start = end = jnp.int32(0)
    for i in range(lengths_ref.shape[0]):
        end = end + lengths_ref[i]
        start = jnp.where(first_row + iota(column, 0) >= end, end, start)
        first_start = jnp.where(first_row >= end, end, first_start)

    def write(g, acc):
        lanes = slice(g * HEAD_WIDTH, (g + 1) * HEAD_WIDTH)
        out = (acc[:, :HEAD_WIDTH] / acc[:, HEAD_WIDTH:]).astype(jnp.bfloat16)
        first_ref[:, lanes] = out[:half]
        second_ref[:, lanes] = out[half:]

    needed = (base >= 0) & (base + span > first_start)

    @pl.when(needed)
    def _():
        k, v = key_ref[...], value_ref[...]
        k = jnp.concatenate([k, k], axis=1)
        v = jnp.concatenate([v, jnp.ones_like(v)], axis=1)
        for t0 in range(0, span, 256):
            s = times_t(heads_ref[...], k[t0 : t0 + 256, :])
            allowed = base + t0 + iota((tok, 256), 1) >= jnp.concatenate([start] * 2, axis=1)
            s = jnp.where(jnp.concatenate([allowed] * groups, axis=0), s, NEG)
            scores_ref[:, t0 : t0 + 256] = s
            top = jnp.maximum(s[:, :HEAD_WIDTH], s[:, HEAD_WIDTH:])
            new_top_ref[...] = jnp.maximum(top, new_top_ref[...] if t0 else top_ref[...])
        for g in range(0, groups, 2):
            rows = slice(g * tok, (g + 2) * tok)
            top = jnp.max(new_top_ref[rows, :], axis=1, keepdims=True)
            top = jnp.broadcast_to(top, (2 * tok, HEAD_WIDTH))
            w = jnp.exp2(scores_ref[rows, :] - jnp.concatenate([top] * reach, axis=1))
            keep = jnp.exp2(top_ref[rows, :] - top)
            acc = times(w.astype(jnp.bfloat16), v)
            acc += acc_ref[rows, :] * jnp.concatenate([keep, keep], axis=1)
            write(g, acc[:tok])
            write(g + 1, acc[tok:])

    @pl.when(jnp.logical_not(needed))
    def _():
        for g in range(groups):
            write(g, acc_ref[g * tok : (g + 1) * tok, :])


def local(queries, keys, values, row_route, lengths):
    n = lax.axis_size("ctx")
    index = lax.axis_index("ctx")
    tok, width = queries.shape
    half = tok // 2
    groups = width // HEAD_WIDTH
    rows = n * SLOTS
    lanes = width + HEAD_WIDTH
    bf16 = jnp.bfloat16
    here = index.astype(jnp.int32).reshape(1)
    even = index % 2 == 0

    packed = pl.pallas_call(
        functools.partial(pack_kernel, n),
        out_shape=jax.ShapeDtypeStruct((rows, lanes), bf16),
        in_specs=[ANY] * 4,
        out_specs=VMEM,
        scratch_shapes=[
            pltpu.VMEM((1, tok), jnp.int32),
            pltpu.VMEM((tok, width), bf16),
            pltpu.VMEM((tok, HEAD_WIDTH), bf16),
            pltpu.VMEM((tok, HEAD_WIDTH), bf16),
            pltpu.SemaphoreType.DMA((4,)),
        ],
        compiler_params=pltpu.CompilerParams(vmem_limit_bytes=60 * 2**20),
        name="pack",
    )(row_route.reshape(1, tok), queries, keys, values)
    got = lax.all_to_all(packed.reshape(n, SLOTS, lanes), "ctx", 0, 0, tiled=True)

    params = pltpu.CompilerParams(vmem_limit_bytes=48 * 2**20)
    part = jax.ShapeDtypeStruct((half, width), bf16)
    my_kv, keep, give = pl.pallas_call(
        functools.partial(unpack_kernel, n),
        out_shape=(jax.ShapeDtypeStruct((tok, 2 * HEAD_WIDTH), bf16), part, part),
        in_specs=[SMEM, VMEM],
        out_specs=(VMEM, VMEM, VMEM),
        compiler_params=params,
        name="unpack",
    )(here, got.reshape(rows, lanes))

    planes = n // PLANE
    groups_of = [list(range(z * PLANE, (z + 1) * PLANE)) for z in range(planes)]
    plane = lax.all_gather(my_kv, "ctx", axis_index_groups=groups_of, axis=0, tiled=True)
    plane = plane.reshape(PLANE, 2, half, 2 * HEAD_WIDTH)
    run = jnp.where(even, plane[:, 0], plane[::-1, 1]).reshape(PLANE * half, 2 * HEAD_WIDTH)
    run_keys, run_values = [run[:, :HEAD_WIDTH]], [run[:, HEAD_WIDTH:]]
    chain = []
    for chip in range(PLANE // 2):
        stops = [z * PLANE + 2 * chip for z in range(planes)]
        stops += [stop + 1 for stop in reversed(stops)]
        chain += list(zip(stops[:-1], stops[1:]))
    for step in range(STEPS):
        run_keys.append(lax.ppermute(run_keys[step], "ctx", chain))
        run_values.append(lax.ppermute(run_values[step], "ctx", chain))

    swap = [(i, i ^ 1) for i in range(n)]
    taken = lax.ppermute(give, "ctx", swap)
    scaled = jax.ShapeDtypeStruct((groups * tok, 2 * HEAD_WIDTH), bf16)
    sums = (
        jax.ShapeDtypeStruct((groups * tok, HEAD_WIDTH), jnp.float32),
        jax.ShapeDtypeStruct((groups * tok, 2 * HEAD_WIDTH), jnp.float32),
    )
    params = pltpu.CompilerParams(vmem_limit_bytes=32 * 2**20)
    pairs = groups * tok * PLANE * half

    def attend(steps, *arrays):
        arrays += tuple(run_keys[step] for step in steps)
        arrays += tuple(run_values[step] for step in steps)
        out = (scaled, *sums) if steps[0] == 0 else sums
        return pl.pallas_call(
            functools.partial(attend_kernel, n, groups, steps),
            out_shape=out,
            in_specs=[SMEM, SMEM] + [VMEM] * len(arrays),
            out_specs=(VMEM,) * len(out),
            scratch_shapes=[pltpu.VMEM((groups * tok, len(steps) * PLANE * half), jnp.float32)],
            compiler_params=params,
            cost_estimate=pl.CostEstimate(
                flops=64 * len(steps) * HEAD_WIDTH * pairs,
                bytes_accessed=2**23,
                transcendentals=8 * len(steps) * pairs,
            ),
            name=f"attend{steps[0]}",
        )(lengths, here, *arrays)

    heads, *state = attend((0,), keep, taken)
    state = (heads, *attend(tuple(range(1, STEPS)), heads, *state))
    first, second = pl.pallas_call(
        functools.partial(finish_kernel, n, groups),
        out_shape=(part, part),
        in_specs=[SMEM, SMEM] + [VMEM] * 5,
        out_specs=(VMEM, VMEM),
        scratch_shapes=[
            pltpu.VMEM((groups * tok, PLANE * half), jnp.float32),
            pltpu.VMEM((groups * tok, HEAD_WIDTH), jnp.float32),
        ],
        compiler_params=params,
        name="finish",
    )(lengths, here, *state, run_keys[STEPS], run_values[STEPS])

    others = lax.all_gather(
        second, "ctx", axis_index_groups=[[i, i + 1] for i in range(0, n, 2)], axis=0
    )
    return jnp.where(
        even,
        jnp.concatenate([first, others[1]], axis=0),
        jnp.concatenate([others[0], first], axis=0),
    )


def solution(mesh):
    placed = (P("ctx", "tp"), P("ctx", "tp"), P("ctx", "tp"), P("ctx"), P())
    return jax.shard_map(
        local, mesh=mesh, in_specs=placed, out_specs=P("ctx", "tp"), check_vma=False
    )
```

```python
import functools
import math

import jax
import jax.numpy as jnp
from jax import lax
from jax.experimental import pallas as pl
from jax.experimental.pallas import tpu as pltpu
from jax.sharding import PartitionSpec as P

HEAD_WIDTH = 128
SLOTS = 8
CAP = 6
PLANE = 8
STEPS = 4
NEG = -1e30
VMEM = pl.BlockSpec(memory_space=pltpu.VMEM)
ANY = pl.BlockSpec(memory_space=pl.ANY)
SMEM = pl.BlockSpec(memory_space=pltpu.SMEM)


def iota(shape, dim):
    return lax.broadcasted_iota(jnp.int32, shape, dim)


def divide(x, by):
    return ((x.astype(jnp.float32) + 0.5) * (1.0 / by)).astype(jnp.int32)


def hot(mask):
    return jnp.where(mask, jnp.float32(1), jnp.float32(0)).astype(jnp.bfloat16)


def times(a, b):
    return jnp.dot(a, b, preferred_element_type=jnp.float32)


def times_t(a, b):
    return lax.dot_general(a, b, (((1,), (1,)), ((), ())), preferred_element_type=jnp.float32)


def pack_kernel(n, route_hbm, q_hbm, k_hbm, v_hbm, out_ref, route_ref, q_ref, k_ref, v_ref, sems):
    copies = [
        pltpu.make_async_copy(src, dst, sems.at[i])
        for i, (src, dst) in enumerate(
            ((route_hbm, route_ref), (k_hbm, k_ref), (v_hbm, v_ref), (q_hbm, q_ref))
        )
    ]
    for copy in copies:
        copy.start()
    tok, width = q_ref.shape
    rows = n * SLOTS
    copies[0].wait()
    route = route_ref[...]
    owner = divide(route, tok)
    slot = route - owner * tok
    square = (tok, tok)
    down, across = iota(square, 0), iota(square, 1)
    route_col = jnp.sum(
        jnp.where(down == across, jnp.broadcast_to(route, square), 0), axis=1, keepdims=True
    )
    owner_col = divide(route_col, tok)
    same = owner_col == jnp.broadcast_to(owner, square)
    order = jnp.sum(jnp.where(same & (down < across), 1, 0), axis=0, keepdims=True)
    order_col = jnp.sum(jnp.where(same & (across < down), 1, 0), axis=1, keepdims=True)
    wide = (rows, tok)
    line = iota(wide, 0)

    def pick(row):
        return hot(line == jnp.broadcast_to(owner * SLOTS + row, wide))

    spare = pick(CAP + (order & 1))
    column = (tok, HEAD_WIDTH)
    order_wide = jnp.broadcast_to(order_col, column)
    place = jnp.where(
        iota(column, 1) == order_wide, (route_col - owner_col * tok + 1).astype(jnp.float32), 0.0
    )
    main = pick(order)
    copies[1].wait()
    copies[2].wait()
    v = v_ref[...].astype(jnp.float32)
    pieces = [jnp.where((order_wide >> 1) == i, v, 0.0) for i in range(3)] + [place]
    extra = times(spare, jnp.concatenate(pieces, axis=1).astype(jnp.bfloat16))
    extra = {
        group: extra[:, i * HEAD_WIDTH : (i + 1) * HEAD_WIDTH]
        for i, group in enumerate((4, 0, 1, 2))
    }
    extra[4] += times(main, k_ref[...])
    copies[3].wait()
    packed = times(main, q_ref[...])
    for group in range(5):
        part = slice(group * HEAD_WIDTH, (group + 1) * HEAD_WIDTH)
        value = extra.get(group)
        if group < 4:
            value = packed[:, part] if value is None else packed[:, part] + value
        out_ref[:, part] = value.astype(jnp.bfloat16)


def unpack_kernel(n, index_ref, got_ref, kv_ref, keep_ref, give_ref):
    rows = n * SLOTS
    tall = (n, rows)
    mark_row = iota(tall, 0) * SLOTS + CAP

    def group(i):
        return got_ref[:, i * HEAD_WIDTH : (i + 1) * HEAD_WIDTH]

    marked = (iota(tall, 1) == mark_row) | (iota(tall, 1) == mark_row + 1)
    marks = times(hot(marked), group(2)).astype(jnp.bfloat16)
    mine = iota(tall, 1) - iota(tall, 0) * SLOTS
    mine = (mine >= 0) & (mine < SLOTS)
    lanes = (HEAD_WIDTH, rows)
    row = iota(lanes, 1) & (SLOTS - 1)

    def place_of(lane):
        spread = times(marks, hot(iota(lanes, 0) == lane))
        return jnp.sum(jnp.where(mine, spread, jnp.float32(0)), axis=0, keepdims=True)

    def pick(place, count, offset):
        wide = (count, rows)
        want = (iota(wide, 0) + 1 + offset).astype(jnp.float32)
        return hot(want == jnp.broadcast_to(place, wide))

    main = place_of(jnp.where(row < CAP, row, -1))
    tok = kv_ref.shape[0]
    kv_ref[:, :HEAD_WIDTH] = times(pick(main, tok, 0), group(4)).astype(jnp.bfloat16)
    v = sum(
        times(pick(place_of(jnp.where(row >= CAP, row - CAP + first, -1)), tok, 0), group(at))
        for at, first in ((4, 0), (0, 2), (1, 4))
    )
    kv_ref[:, HEAD_WIDTH:] = v.astype(jnp.bfloat16)
    half, width = keep_ref.shape
    even = index_ref[0] % 2 == 0
    for ref, own in ((keep_ref, even), (give_ref, jnp.logical_not(even))):
        chosen = pick(main, half, jnp.where(own, 0, half))
        ref[...] = times(chosen, got_ref[:, :width]).astype(jnp.bfloat16)


def attend_kernel(n, groups, steps, lengths_ref, index_ref, *refs):
    count = len(steps)
    begin = steps[0] == 0
    given = 2 if begin else 3
    key_refs = dict(zip(steps, refs[given : given + count]))
    value_refs = dict(zip(steps, refs[given + count : given + 2 * count]))
    if begin:
        q1_ref, q2_ref = refs[:given]
        heads_ref, top_ref, acc_ref, scores_ref = refs[given + 2 * count :]
    else:
        heads_ref, old_top_ref, old_acc_ref = refs[:given]
        top_ref, acc_ref, scores_ref = refs[given + 2 * count :]
    tok = heads_ref.shape[0] // groups
    half = tok // 2
    span = key_refs[steps[0]].shape[0]
    index = index_ref[0]
    chunk = jnp.where(index % 2 == 0, index // 2, n - 1 - index // 2)
    first_row = chunk * tok
    run = first_row // span

    if begin:
        scale = HEAD_WIDTH ** (-0.5) * math.log2(math.e)
        for g in range(groups):
            lanes = slice(g * HEAD_WIDTH, (g + 1) * HEAD_WIDTH)
            for ref, at in ((q1_ref, g * tok), (q2_ref, g * tok + half)):
                scaled = ref[:, lanes].astype(jnp.float32) * scale
                upper = scaled.astype(jnp.bfloat16)
                lower = (scaled - upper.astype(jnp.float32)).astype(jnp.bfloat16)
                heads_ref[at : at + half, :HEAD_WIDTH] = upper
                heads_ref[at : at + half, HEAD_WIDTH:] = lower
    else:
        top_ref[...] = old_top_ref[...]

    column = (tok, HEAD_WIDTH)
    query_pos = first_row + iota(column, 0)
    start = jnp.zeros(column, jnp.int32)
    first_start = last_start = end = jnp.int32(0)
    for i in range(lengths_ref.shape[0]):
        end = end + lengths_ref[i]
        start = jnp.where(query_pos >= end, end, start)
        first_start = jnp.where(first_row >= end, end, first_start)
        last_start = jnp.where(first_row + tok - 1 >= end, end, last_start)

    def score(step, base, masked):
        k = key_refs[step][...]
        k = jnp.concatenate([k, k], axis=1)
        reach = span // HEAD_WIDTH
        if masked:
            key_pos = base + iota((tok, span), 1)
            allowed = key_pos >= jnp.concatenate([start] * reach, axis=1)
            if step == 0:
                allowed &= key_pos <= jnp.concatenate([query_pos] * reach, axis=1)
        for t0 in range(0, span, 256):
            s = times_t(heads_ref[...], k[t0 : t0 + 256, :])
            if masked:
                part = allowed[:, t0 : t0 + 256]
                s = jnp.where(jnp.concatenate([part] * groups, axis=0), s, NEG)
            at = (step - steps[0]) * span + t0
            scores_ref[:, at : at + 256] = s
            top = jnp.maximum(s[:, :HEAD_WIDTH], s[:, HEAD_WIDTH:])
            if step or t0:
                top = jnp.maximum(top, top_ref[...])
            top_ref[...] = top

    def weigh(step):
        v = value_refs[step][...]
        v = jnp.concatenate([v, jnp.ones_like(v)], axis=1)
        at = (step - steps[0]) * span
        for r0 in range(0, groups * tok, 2 * tok):
            rows = slice(r0, r0 + 2 * tok)
            top = jnp.concatenate([top_ref[rows, :]] * (span // HEAD_WIDTH), axis=1)
            w = jnp.exp2(scores_ref[rows, at : at + span] - top)
            acc = times(w.astype(jnp.bfloat16), v)
            if step:
                acc += acc_ref[rows, :]
            acc_ref[rows, :] = acc

    def base_of(step):
        return (run - step) * span

    def needed(step):
        return (base_of(step) >= 0) & (base_of(step) + span > first_start)

    for step in steps:
        if step == 0:
            score(0, base_of(0), True)
            continue
        clear = base_of(step) >= last_start

        @pl.when(needed(step) & clear)
        def _(step=step):
            score(step, base_of(step), False)

        @pl.when(needed(step) & jnp.logical_not(clear))
        def _(step=step):
            score(step, base_of(step), True)

    def settle():
        for g in range(groups):
            rows = slice(g * tok, (g + 1) * tok)
            top = jnp.max(top_ref[rows, :], axis=1, keepdims=True)
            top = jnp.broadcast_to(top, column)
            top_ref[rows, :] = top
            if not begin:
                keep = jnp.exp2(old_top_ref[rows, :] - top)
                acc_ref[rows, :] = old_acc_ref[rows, :] * jnp.concatenate([keep, keep], axis=1)

    if begin:
        settle()
    else:
        pl.when(needed(steps[0]))(settle)

        @pl.when(jnp.logical_not(needed(steps[0])))
        def _():
            acc_ref[...] = old_acc_ref[...]

    for step in steps:
        if step == 0:
            weigh(0)
        else:

            @pl.when(needed(step))
            def _(step=step):
                weigh(step)


def reach_of(n, tok, span, lengths_ref, index_ref):
    index = index_ref[0]
    first_row = jnp.where(index % 2 == 0, index // 2, n - 1 - index // 2) * tok
    first_start = end = jnp.int32(0)
    for i in range(lengths_ref.shape[0]):
        end = end + lengths_ref[i]
        first_start = jnp.where(first_row >= end, end, first_start)
    base = (first_row // span - STEPS) * span
    return first_row, base, (base >= 0) & (base + span > first_start)


def far_score_kernel(n, groups, lengths_ref, index_ref, heads_ref, old_top_ref, key_ref, scores_ref, top_ref):
    tok = heads_ref.shape[0] // groups
    span = key_ref.shape[0]
    first_row, base, needed = reach_of(n, tok, span, lengths_ref, index_ref)

    @pl.when(needed)
    def _():
        column = (tok, HEAD_WIDTH)
        start = jnp.zeros(column, jnp.int32)
        end = jnp.int32(0)
        for i in range(lengths_ref.shape[0]):
            end = end + lengths_ref[i]
            start = jnp.where(first_row + iota(column, 0) >= end, end, start)
        k = key_ref[...]
        k = jnp.concatenate([k, k], axis=1)
        for t0 in range(0, span, 256):
            s = times_t(heads_ref[...], k[t0 : t0 + 256, :])
            allowed = base + t0 + iota((tok, 256), 1) >= jnp.concatenate([start] * 2, axis=1)
            s = jnp.where(jnp.concatenate([allowed] * groups, axis=0), s, NEG)
            scores_ref[:, t0 : t0 + 256] = s
            top = jnp.maximum(s[:, :HEAD_WIDTH], s[:, HEAD_WIDTH:])
            top_ref[...] = jnp.maximum(top, top_ref[...] if t0 else old_top_ref[...])
        for g in range(groups):
            rows = slice(g * tok, (g + 1) * tok)
            top = jnp.max(top_ref[rows, :], axis=1, keepdims=True)
            top_ref[rows, :] = jnp.broadcast_to(top, column)

    @pl.when(jnp.logical_not(needed))
    def _():
        top_ref[...] = old_top_ref[...]


def finish_kernel(
    n, groups, lengths_ref, index_ref, value_ref, scores_ref, old_top_ref, top_ref, acc_ref, first_ref, second_ref
):
    tok = acc_ref.shape[0] // groups
    half = tok // 2
    span = value_ref.shape[0]
    _, _, needed = reach_of(n, tok, span, lengths_ref, index_ref)

    def write(g, acc):
        lanes = slice(g * HEAD_WIDTH, (g + 1) * HEAD_WIDTH)
        out = (acc[:, :HEAD_WIDTH] / acc[:, HEAD_WIDTH:]).astype(jnp.bfloat16)
        first_ref[:, lanes] = out[:half]
        second_ref[:, lanes] = out[half:]

    @pl.when(needed)
    def _():
        v = value_ref[...]
        v = jnp.concatenate([v, jnp.ones_like(v)], axis=1)
        for g in range(0, groups, 2):
            rows = slice(g * tok, (g + 2) * tok)
            top = top_ref[rows, :]
            w = jnp.exp2(scores_ref[rows, :] - jnp.concatenate([top] * (span // HEAD_WIDTH), axis=1))
            keep = jnp.exp2(old_top_ref[rows, :] - top)
            acc = times(w.astype(jnp.bfloat16), v)
            acc += acc_ref[rows, :] * jnp.concatenate([keep, keep], axis=1)
            write(g, acc[:tok])
            write(g + 1, acc[tok:])

    @pl.when(jnp.logical_not(needed))
    def _():
        for g in range(groups):
            write(g, acc_ref[g * tok : (g + 1) * tok, :])


def local(queries, keys, values, row_route, lengths):
    n = lax.axis_size("ctx")
    index = lax.axis_index("ctx")
    tok, width = queries.shape
    half = tok // 2
    groups = width // HEAD_WIDTH
    rows = n * SLOTS
    lanes = width + HEAD_WIDTH
    bf16 = jnp.bfloat16
    here = index.astype(jnp.int32).reshape(1)
    even = index % 2 == 0

    packed = pl.pallas_call(
        functools.partial(pack_kernel, n),
        out_shape=jax.ShapeDtypeStruct((rows, lanes), bf16),
        in_specs=[ANY] * 4,
        out_specs=VMEM,
        scratch_shapes=[
            pltpu.VMEM((1, tok), jnp.int32),
            pltpu.VMEM((tok, width), bf16),
            pltpu.VMEM((tok, HEAD_WIDTH), bf16),
            pltpu.VMEM((tok, HEAD_WIDTH), bf16),
            pltpu.SemaphoreType.DMA((4,)),
        ],
        compiler_params=pltpu.CompilerParams(vmem_limit_bytes=60 * 2**20),
        name="pack",
    )(row_route.reshape(1, tok), queries, keys, values)
    got = lax.all_to_all(packed.reshape(n, SLOTS, lanes), "ctx", 0, 0, tiled=True)

    params = pltpu.CompilerParams(vmem_limit_bytes=48 * 2**20)
    part = jax.ShapeDtypeStruct((half, width), bf16)
    my_kv, keep, give = pl.pallas_call(
        functools.partial(unpack_kernel, n),
        out_shape=(jax.ShapeDtypeStruct((tok, 2 * HEAD_WIDTH), bf16), part, part),
        in_specs=[SMEM, VMEM],
        out_specs=(VMEM, VMEM, VMEM),
        compiler_params=params,
        name="unpack",
    )(here, got.reshape(rows, lanes))

    planes = n // PLANE
    groups_of = [list(range(z * PLANE, (z + 1) * PLANE)) for z in range(planes)]
    plane = lax.all_gather(my_kv, "ctx", axis_index_groups=groups_of, axis=0, tiled=True)
    plane = plane.reshape(PLANE, 2, half, 2 * HEAD_WIDTH)
    run = jnp.where(even, plane[:, 0], plane[::-1, 1]).reshape(PLANE * half, 2 * HEAD_WIDTH)
    run_keys, run_values = [run[:, :HEAD_WIDTH]], [run[:, HEAD_WIDTH:]]
    chain = []
    for chip in range(PLANE // 2):
        stops = [z * PLANE + 2 * chip for z in range(planes)]
        stops += [stop + 1 for stop in reversed(stops)]
        chain += list(zip(stops[:-1], stops[1:]))
    for step in range(STEPS):
        run_keys.append(lax.ppermute(run_keys[step], "ctx", chain))
        run_values.append(lax.ppermute(run_values[step], "ctx", chain))

    swap = [(i, i ^ 1) for i in range(n)]
    taken = lax.ppermute(give, "ctx", swap)
    scaled = jax.ShapeDtypeStruct((groups * tok, 2 * HEAD_WIDTH), bf16)
    sums = (
        jax.ShapeDtypeStruct((groups * tok, HEAD_WIDTH), jnp.float32),
        jax.ShapeDtypeStruct((groups * tok, 2 * HEAD_WIDTH), jnp.float32),
    )
    params = pltpu.CompilerParams(vmem_limit_bytes=32 * 2**20)
    pairs = groups * tok * PLANE * half

    def attend(steps, *arrays):
        arrays += tuple(run_keys[step] for step in steps)
        arrays += tuple(run_values[step] for step in steps)
        out = (scaled, *sums) if steps[0] == 0 else sums
        return pl.pallas_call(
            functools.partial(attend_kernel, n, groups, steps),
            out_shape=out,
            in_specs=[SMEM, SMEM] + [VMEM] * len(arrays),
            out_specs=(VMEM,) * len(out),
            scratch_shapes=[pltpu.VMEM((groups * tok, len(steps) * PLANE * half), jnp.float32)],
            compiler_params=params,
            cost_estimate=pl.CostEstimate(
                flops=64 * len(steps) * HEAD_WIDTH * pairs,
                bytes_accessed=2**23,
                transcendentals=8 * len(steps) * pairs,
            ),
            name=f"attend{steps[0]}",
        )(lengths, here, *arrays)

    heads, *state = attend((0,), keep, taken)
    top, acc = attend(tuple(range(1, STEPS)), heads, *state)
    scores, new_top = pl.pallas_call(
        functools.partial(far_score_kernel, n, groups),
        out_shape=(jax.ShapeDtypeStruct((groups * tok, PLANE * half), jnp.float32), sums[0]),
        in_specs=[SMEM, SMEM] + [VMEM] * 3,
        out_specs=(VMEM, VMEM),
        compiler_params=params,
        name="far_score",
    )(lengths, here, heads, top, run_keys[STEPS])
    first, second = pl.pallas_call(
        functools.partial(finish_kernel, n, groups),
        out_shape=(part, part),
        in_specs=[SMEM, SMEM] + [VMEM] * 5,
        out_specs=(VMEM, VMEM),
        compiler_params=params,
        name="finish",
    )(lengths, here, run_values[STEPS], scores, top, new_top, acc)

    others = lax.all_gather(
        second, "ctx", axis_index_groups=[[i, i + 1] for i in range(0, n, 2)], axis=0
    )
    return jnp.where(
        even,
        jnp.concatenate([first, others[1]], axis=0),
        jnp.concatenate([others[0], first], axis=0),
    )


def solution(mesh):
    placed = (P("ctx", "tp"), P("ctx", "tp"), P("ctx", "tp"), P("ctx"), P())
    return jax.shard_map(
        local, mesh=mesh, in_specs=placed, out_specs=P("ctx", "tp"), check_vma=False
    )
```

```python
import functools
import math

import jax
import jax.numpy as jnp
from jax import lax
from jax.experimental import pallas as pl
from jax.experimental.pallas import tpu as pltpu
from jax.sharding import PartitionSpec as P

HEAD_WIDTH = 128
SLOTS = 8
CAP = 6
PLANE = 8
STEPS = 4
NEG = -1e30
VMEM = pl.BlockSpec(memory_space=pltpu.VMEM)
ANY = pl.BlockSpec(memory_space=pl.ANY)
SMEM = pl.BlockSpec(memory_space=pltpu.SMEM)


def iota(shape, dim):
    return lax.broadcasted_iota(jnp.int32, shape, dim)


def divide(x, by):
    return ((x.astype(jnp.float32) + 0.5) * (1.0 / by)).astype(jnp.int32)


def hot(mask):
    return jnp.where(mask, jnp.float32(1), jnp.float32(0)).astype(jnp.bfloat16)


def times(a, b):
    return jnp.dot(a, b, preferred_element_type=jnp.float32)


def times_t(a, b):
    return lax.dot_general(a, b, (((1,), (1,)), ((), ())), preferred_element_type=jnp.float32)


def pack_kernel(n, route_hbm, q_hbm, k_hbm, v_hbm, out_ref, route_ref, q_ref, k_ref, v_ref, sems):
    copies = [
        pltpu.make_async_copy(src, dst, sems.at[i])
        for i, (src, dst) in enumerate(
            ((route_hbm, route_ref), (k_hbm, k_ref), (v_hbm, v_ref), (q_hbm, q_ref))
        )
    ]
    for copy in copies:
        copy.start()
    tok, width = q_ref.shape
    rows = n * SLOTS
    copies[0].wait()
    route = route_ref[...]
    owner = divide(route, tok)
    slot = route - owner * tok
    square = (tok, tok)
    down, across = iota(square, 0), iota(square, 1)
    route_col = jnp.sum(
        jnp.where(down == across, jnp.broadcast_to(route, square), 0), axis=1, keepdims=True
    )
    owner_col = divide(route_col, tok)
    same = owner_col == jnp.broadcast_to(owner, square)
    order = jnp.sum(jnp.where(same & (down < across), 1, 0), axis=0, keepdims=True)
    order_col = jnp.sum(jnp.where(same & (across < down), 1, 0), axis=1, keepdims=True)
    wide = (rows, tok)
    line = iota(wide, 0)

    def pick(row):
        return hot(line == jnp.broadcast_to(owner * SLOTS + row, wide))

    spare = pick(CAP + (order & 1))
    column = (tok, HEAD_WIDTH)
    order_wide = jnp.broadcast_to(order_col, column)
    place = jnp.where(
        iota(column, 1) == order_wide, (route_col - owner_col * tok + 1).astype(jnp.float32), 0.0
    )
    main = pick(order)
    copies[1].wait()
    copies[2].wait()
    v = v_ref[...].astype(jnp.float32)
    pieces = [jnp.where((order_wide >> 1) == i, v, 0.0) for i in range(3)] + [place]
    extra = times(spare, jnp.concatenate(pieces, axis=1).astype(jnp.bfloat16))
    extra = {
        group: extra[:, i * HEAD_WIDTH : (i + 1) * HEAD_WIDTH]
        for i, group in enumerate((4, 0, 1, 2))
    }
    extra[4] += times(main, k_ref[...])
    copies[3].wait()
    packed = times(main, q_ref[...])
    for group in range(5):
        part = slice(group * HEAD_WIDTH, (group + 1) * HEAD_WIDTH)
        value = extra.get(group)
        if group < 4:
            value = packed[:, part] if value is None else packed[:, part] + value
        out_ref[:, part] = value.astype(jnp.bfloat16)


def unpack_kernel(n, index_ref, got_ref, kv_ref, keep_ref, give_ref):
    rows = n * SLOTS
    tall = (n, rows)
    mark_row = iota(tall, 0) * SLOTS + CAP

    def group(i):
        return got_ref[:, i * HEAD_WIDTH : (i + 1) * HEAD_WIDTH]

    marked = (iota(tall, 1) == mark_row) | (iota(tall, 1) == mark_row + 1)
    marks = times(hot(marked), group(2)).astype(jnp.bfloat16)
    mine = iota(tall, 1) - iota(tall, 0) * SLOTS
    mine = (mine >= 0) & (mine < SLOTS)
    lanes = (HEAD_WIDTH, rows)
    row = iota(lanes, 1) & (SLOTS - 1)

    def place_of(lane):
        spread = times(marks, hot(iota(lanes, 0) == lane))
        return jnp.sum(jnp.where(mine, spread, jnp.float32(0)), axis=0, keepdims=True)

    def pick(place, count, offset):
        wide = (count, rows)
        want = (iota(wide, 0) + 1 + offset).astype(jnp.float32)
        return hot(want == jnp.broadcast_to(place, wide))

    main = place_of(jnp.where(row < CAP, row, -1))
    tok = kv_ref.shape[0]
    kv_ref[:, :HEAD_WIDTH] = times(pick(main, tok, 0), group(4)).astype(jnp.bfloat16)
    v = sum(
        times(pick(place_of(jnp.where(row >= CAP, row - CAP + first, -1)), tok, 0), group(at))
        for at, first in ((4, 0), (0, 2), (1, 4))
    )
    kv_ref[:, HEAD_WIDTH:] = v.astype(jnp.bfloat16)
    half, width = keep_ref.shape
    even = index_ref[0] % 2 == 0
    for ref, own in ((keep_ref, even), (give_ref, jnp.logical_not(even))):
        chosen = pick(main, half, jnp.where(own, 0, half))
        ref[...] = times(chosen, got_ref[:, :width]).astype(jnp.bfloat16)


def attend_kernel(n, groups, steps, lengths_ref, index_ref, *refs):
    count = len(steps)
    begin = steps[0] == 0
    given = 2 if begin else 3
    key_refs = dict(zip(steps, refs[given : given + count]))
    value_refs = dict(zip(steps, refs[given + count : given + 2 * count]))
    if begin:
        q1_ref, q2_ref = refs[:given]
        heads_ref, top_ref, acc_ref, scores_ref = refs[given + 2 * count :]
    else:
        heads_ref, old_top_ref, old_acc_ref = refs[:given]
        top_ref, acc_ref, scores_ref = refs[given + 2 * count :]
    tok = heads_ref.shape[0] // groups
    half = tok // 2
    span = key_refs[steps[0]].shape[0]
    index = index_ref[0]
    chunk = jnp.where(index % 2 == 0, index // 2, n - 1 - index // 2)
    first_row = chunk * tok
    run = first_row // span

    if begin:
        scale = HEAD_WIDTH ** (-0.5) * math.log2(math.e)
        for g in range(groups):
            lanes = slice(g * HEAD_WIDTH, (g + 1) * HEAD_WIDTH)
            for ref, at in ((q1_ref, g * tok), (q2_ref, g * tok + half)):
                scaled = ref[:, lanes].astype(jnp.float32) * scale
                upper = scaled.astype(jnp.bfloat16)
                lower = (scaled - upper.astype(jnp.float32)).astype(jnp.bfloat16)
                heads_ref[at : at + half, :HEAD_WIDTH] = upper
                heads_ref[at : at + half, HEAD_WIDTH:] = lower
    else:
        top_ref[...] = old_top_ref[...]

    column = (tok, HEAD_WIDTH)
    query_pos = first_row + iota(column, 0)
    start = jnp.zeros(column, jnp.int32)
    first_start = last_start = end = jnp.int32(0)
    for i in range(lengths_ref.shape[0]):
        end = end + lengths_ref[i]
        start = jnp.where(query_pos >= end, end, start)
        first_start = jnp.where(first_row >= end, end, first_start)
        last_start = jnp.where(first_row + tok - 1 >= end, end, last_start)

    def score(step, base, masked):
        k = key_refs[step][...]
        k = jnp.concatenate([k, k], axis=1)
        reach = span // HEAD_WIDTH
        if masked:
            key_pos = base + iota((tok, span), 1)
            allowed = key_pos >= jnp.concatenate([start] * reach, axis=1)
            if step == 0:
                allowed &= key_pos <= jnp.concatenate([query_pos] * reach, axis=1)
        for t0 in range(0, span, 256):
            s = times_t(heads_ref[...], k[t0 : t0 + 256, :])
            if masked:
                part = allowed[:, t0 : t0 + 256]
                s = jnp.where(jnp.concatenate([part] * groups, axis=0), s, NEG)
            at = (step - steps[0]) * span + t0
            scores_ref[:, at : at + 256] = s
            top = jnp.maximum(s[:, :HEAD_WIDTH], s[:, HEAD_WIDTH:])
            if step or t0:
                top = jnp.maximum(top, top_ref[...])
            top_ref[...] = top

    def weigh(step):
        v = value_refs[step][...]
        v = jnp.concatenate([v, jnp.ones_like(v)], axis=1)
        at = (step - steps[0]) * span
        for r0 in range(0, groups * tok, 2 * tok):
            rows = slice(r0, r0 + 2 * tok)
            top = jnp.concatenate([top_ref[rows, :]] * (span // HEAD_WIDTH), axis=1)
            w = jnp.exp2(scores_ref[rows, at : at + span] - top)
            acc = times(w.astype(jnp.bfloat16), v)
            if step:
                acc += acc_ref[rows, :]
            acc_ref[rows, :] = acc

    def base_of(step):
        return (run - step) * span

    def needed(step):
        return (base_of(step) >= 0) & (base_of(step) + span > first_start)

    for step in steps:
        if step == 0:
            score(0, base_of(0), True)
            continue
        clear = base_of(step) >= last_start

        @pl.when(needed(step) & clear)
        def _(step=step):
            score(step, base_of(step), False)

        @pl.when(needed(step) & jnp.logical_not(clear))
        def _(step=step):
            score(step, base_of(step), True)

    def settle():
        for g in range(groups):
            rows = slice(g * tok, (g + 1) * tok)
            top = jnp.max(top_ref[rows, :], axis=1, keepdims=True)
            top = jnp.broadcast_to(top, column)
            top_ref[rows, :] = top
            if not begin:
                keep = jnp.exp2(old_top_ref[rows, :] - top)
                acc_ref[rows, :] = old_acc_ref[rows, :] * jnp.concatenate([keep, keep], axis=1)

    if begin:
        settle()
    else:
        pl.when(needed(steps[0]))(settle)

        @pl.when(jnp.logical_not(needed(steps[0])))
        def _():
            acc_ref[...] = old_acc_ref[...]

    for step in steps:
        if step == 0:
            weigh(0)
        else:

            @pl.when(needed(step))
            def _(step=step):
                weigh(step)


def reach_of(n, tok, span, lengths_ref, index_ref):
    index = index_ref[0]
    first_row = jnp.where(index % 2 == 0, index // 2, n - 1 - index // 2) * tok
    first_start = end = jnp.int32(0)
    for i in range(lengths_ref.shape[0]):
        end = end + lengths_ref[i]
        first_start = jnp.where(first_row >= end, end, first_start)
    base = (first_row // span - STEPS) * span
    return first_row, base, (base >= 0) & (base + span > first_start)


def far_score_kernel(n, groups, lengths_ref, index_ref, heads_ref, old_top_ref, key_ref, scores_ref, top_ref):
    tok = heads_ref.shape[0] // groups
    span = key_ref.shape[0]
    first_row, base, needed = reach_of(n, tok, span, lengths_ref, index_ref)

    @pl.when(needed)
    def _():
        column = (tok, HEAD_WIDTH)
        start = jnp.zeros(column, jnp.int32)
        end = jnp.int32(0)
        for i in range(lengths_ref.shape[0]):
            end = end + lengths_ref[i]
            start = jnp.where(first_row + iota(column, 0) >= end, end, start)
        k = key_ref[...]
        k = jnp.concatenate([k, k], axis=1)
        for t0 in range(0, span, 256):
            s = times_t(heads_ref[...], k[t0 : t0 + 256, :])
            allowed = base + t0 + iota((tok, 256), 1) >= jnp.concatenate([start] * 2, axis=1)
            s = jnp.where(jnp.concatenate([allowed] * groups, axis=0), s, NEG)
            scores_ref[:, t0 : t0 + 256] = s
            top = jnp.maximum(s[:, :HEAD_WIDTH], s[:, HEAD_WIDTH:])
            top_ref[...] = jnp.maximum(top, top_ref[...] if t0 else old_top_ref[...])
        for g in range(groups):
            rows = slice(g * tok, (g + 1) * tok)
            top = jnp.max(top_ref[rows, :], axis=1, keepdims=True)
            top_ref[rows, :] = jnp.broadcast_to(top, column)

    @pl.when(jnp.logical_not(needed))
    def _():
        top_ref[...] = old_top_ref[...]


def finish_kernel(
    n, groups, lengths_ref, index_ref, value_ref, scores_ref, old_top_ref, top_ref, acc_ref, first_ref, second_ref
):
    tok = acc_ref.shape[0] // groups
    half = tok // 2
    span = value_ref.shape[0]
    _, _, needed = reach_of(n, tok, span, lengths_ref, index_ref)

    def write(g, acc):
        lanes = slice(g * HEAD_WIDTH, (g + 1) * HEAD_WIDTH)
        out = (acc[:, :HEAD_WIDTH] / acc[:, HEAD_WIDTH:]).astype(jnp.bfloat16)
        first_ref[:, lanes] = out[:half]
        second_ref[:, lanes] = out[half:]

    @pl.when(needed)
    def _():
        v = value_ref[...]
        v = jnp.concatenate([v, jnp.ones_like(v)], axis=1)
        for g in range(0, groups, 2):
            rows = slice(g * tok, (g + 2) * tok)
            top = top_ref[rows, :]
            w = jnp.exp2(scores_ref[rows, :] - jnp.concatenate([top] * (span // HEAD_WIDTH), axis=1))
            keep = jnp.exp2(old_top_ref[rows, :] - top)
            acc = times(w.astype(jnp.bfloat16), v)
            acc += acc_ref[rows, :] * jnp.concatenate([keep, keep], axis=1)
            write(g, acc[:tok])
            write(g + 1, acc[tok:])

    @pl.when(jnp.logical_not(needed))
    def _():
        for g in range(groups):
            write(g, acc_ref[g * tok : (g + 1) * tok, :])


def local(queries, keys, values, row_route, lengths):
    n = lax.axis_size("ctx")
    index = lax.axis_index("ctx")
    tok, width = queries.shape
    half = tok // 2
    groups = width // HEAD_WIDTH
    rows = n * SLOTS
    lanes = width + HEAD_WIDTH
    bf16 = jnp.bfloat16
    here = index.astype(jnp.int32).reshape(1)
    even = index % 2 == 0

    packed = pl.pallas_call(
        functools.partial(pack_kernel, n),
        out_shape=jax.ShapeDtypeStruct((rows, lanes), bf16),
        in_specs=[ANY] * 4,
        out_specs=VMEM,
        scratch_shapes=[
            pltpu.VMEM((1, tok), jnp.int32),
            pltpu.VMEM((tok, width), bf16),
            pltpu.VMEM((tok, HEAD_WIDTH), bf16),
            pltpu.VMEM((tok, HEAD_WIDTH), bf16),
            pltpu.SemaphoreType.DMA((4,)),
        ],
        compiler_params=pltpu.CompilerParams(vmem_limit_bytes=60 * 2**20),
        name="pack",
    )(row_route.reshape(1, tok), queries, keys, values)
    got = lax.all_to_all(packed.reshape(n, SLOTS, lanes), "ctx", 0, 0, tiled=True)

    params = pltpu.CompilerParams(vmem_limit_bytes=48 * 2**20)
    part = jax.ShapeDtypeStruct((half, width), bf16)
    my_kv, keep, give = pl.pallas_call(
        functools.partial(unpack_kernel, n),
        out_shape=(jax.ShapeDtypeStruct((tok, 2 * HEAD_WIDTH), bf16), part, part),
        in_specs=[SMEM, VMEM],
        out_specs=(VMEM, VMEM, VMEM),
        compiler_params=params,
        name="unpack",
    )(here, got.reshape(rows, lanes))

    planes = n // PLANE
    groups_of = [list(range(z * PLANE, (z + 1) * PLANE)) for z in range(planes)]
    plane = lax.all_gather(my_kv, "ctx", axis_index_groups=groups_of, axis=0, tiled=True)
    plane = plane.reshape(PLANE, 2, half, 2 * HEAD_WIDTH)
    run = jnp.where(even, plane[:, 0], plane[::-1, 1]).reshape(PLANE * half, 2 * HEAD_WIDTH)
    run_keys, run_values = [run[:, :HEAD_WIDTH]], [run[:, HEAD_WIDTH:]]
    chain = []
    for chip in range(PLANE // 2):
        stops = [z * PLANE + 2 * chip for z in range(planes)]
        stops += [stop + 1 for stop in reversed(stops)]
        chain += list(zip(stops[:-1], stops[1:]))
    for step in range(STEPS):
        run_keys.append(lax.ppermute(run_keys[step], "ctx", chain))
        run_values.append(lax.ppermute(run_values[step], "ctx", chain))

    swap = [(i, i ^ 1) for i in range(n)]
    taken = lax.ppermute(give, "ctx", swap)
    scaled = jax.ShapeDtypeStruct((groups * tok, 2 * HEAD_WIDTH), bf16)
    sums = (
        jax.ShapeDtypeStruct((groups * tok, HEAD_WIDTH), jnp.float32),
        jax.ShapeDtypeStruct((groups * tok, 2 * HEAD_WIDTH), jnp.float32),
    )
    params = pltpu.CompilerParams(vmem_limit_bytes=32 * 2**20)
    pairs = groups * tok * PLANE * half

    def attend(steps, *arrays):
        arrays += tuple(run_keys[step] for step in steps)
        arrays += tuple(run_values[step] for step in steps)
        out = (scaled, *sums) if steps[0] == 0 else sums
        return pl.pallas_call(
            functools.partial(attend_kernel, n, groups, steps),
            out_shape=out,
            in_specs=[SMEM, SMEM] + [VMEM] * len(arrays),
            out_specs=(VMEM,) * len(out),
            scratch_shapes=[pltpu.VMEM((groups * tok, len(steps) * PLANE * half), jnp.float32)],
            compiler_params=params,
            cost_estimate=pl.CostEstimate(
                flops=64 * len(steps) * HEAD_WIDTH * pairs,
                bytes_accessed=2**23,
                transcendentals=8 * len(steps) * pairs,
            ),
            name=f"attend{steps[0]}",
        )(lengths, here, *arrays)

    heads, *state = attend((0,), keep, taken)
    top, acc = attend(tuple(range(1, STEPS)), heads, *state)
    scores, new_top = pl.pallas_call(
        functools.partial(far_score_kernel, n, groups),
        out_shape=(jax.ShapeDtypeStruct((groups * tok, PLANE * half), jnp.float32), sums[0]),
        in_specs=[SMEM, SMEM] + [VMEM] * 3,
        out_specs=(VMEM, VMEM),
        compiler_params=params,
        name="far_score",
    )(lengths, here, heads, top, run_keys[STEPS])
    first, second = pl.pallas_call(
        functools.partial(finish_kernel, n, groups),
        out_shape=(part, part),
        in_specs=[SMEM, SMEM] + [VMEM] * 5,
        out_specs=(VMEM, VMEM),
        compiler_params=params,
        name="finish",
    )(lengths, here, run_values[STEPS], scores, top, new_top, acc)

    others = lax.all_gather(
        second, "ctx", axis_index_groups=[[i, i + 1] for i in range(0, n, 2)], axis=0
    )
    return lax.dynamic_update_slice(
        others.reshape(tok, width), first, (jnp.where(even, 0, half), 0)
    )


def solution(mesh):
    placed = (P("ctx", "tp"), P("ctx", "tp"), P("ctx", "tp"), P("ctx"), P())
    return jax.shard_map(
        local, mesh=mesh, in_specs=placed, out_specs=P("ctx", "tp"), check_vma=False
    )
```
